512 devices in a mesh: gx: 32 (over z, core), gy: 16 (over x, y).
Axes of the slice: x: 4, y: 4, z: 16, core: 2. Of those that a mesh axis runs over, the one named last changes fastest.
Arguments:
- send_owner: int32 [32, 16, 32], P('gx', 'gy'), may hold values from 0 to 16, as said below
- send_box: int32 [32, 16, 32], P('gx', 'gy'), may hold values from 0 to 3, as said below
- rho_old: float32 [32, 16, 32, 8, 1024], P('gx', 'gy'), may hold values from 0.15 to 1.2
- rhs_old: float32 [32, 16, 32, 8, 1024], P('gx', 'gy'), may hold values from -6 to 6
Outputs:
- phi: float32 [8, 1024, 2048], P(None, 'gx', 'gy')
The draws below stay inside these ranges and needn't reach their ends.
Inputs may be any that keep to these rules, and one draw needn't show every extreme that they name: `send_owner`: in each gx row, every box of every new owner is named by exactly one slot; no old owner gives more than 2 boxes to one new owner, and in every row one old owner gives exactly 2 to every new owner. 16 marks an empty slot. `send_box`: empty slots hold 0.
All inputs are finite; a program needn't handle non-finite values.
Results may differ from the reference program's by a relative error of at most 0.00027.
Values sent between devices are 32-bit elements; how exact they have to be, the bound alone decides.
A program may use at most 128 MiB of HBM per device.

```python
import math
import jax
import jax.numpy as jnp
from jax import lax

CX = 32
CY = 128
NZ = 8
BS = 32
BOTTOM = 6
CYCLES = 2
BOX_DEV = 4
CAP = 2
OLD_SLOTS = 32
NX = 1024
NY = 2048
N_GX = 32
N_GY = 16


def regrid_tables(key):
    subkeys = jax.random.split(key, 5)
    tickets = CAP * N_GY
    queue = N_GY * BOX_DEV
    hot_sender = jax.random.randint(subkeys[0], (N_GX,), 0, N_GY)
    ticket_sender = jnp.arange(tickets, dtype=jnp.int32) // CAP
    sender_level = jax.random.randint(subkeys[1], (N_GX, N_GY), 0, 4)
    sender_level = jnp.where(jnp.arange(N_GY)[None, :] == hot_sender[:, None], 8, sender_level)
    ticket_level = jnp.take(sender_level, ticket_sender, axis=1)
    base_score = jax.random.randint(subkeys[2], (N_GX, N_GY, tickets), 0, 4096)
    ticket_score = (ticket_level[:, None, :] * 4096 + base_score) * tickets + jnp.arange(tickets, dtype=jnp.int32)
    unused, chosen = lax.top_k(ticket_score, BOX_DEV)
    sender_of = (chosen // CAP).reshape(N_GX, queue).astype(jnp.int32)
    random_key = jax.random.randint(subkeys[3], (N_GX, queue), 0, 4096) * queue + jnp.arange(queue, dtype=jnp.int32)
    sort_order = jnp.argsort(sender_of * (4096 * queue) + random_key, axis=1)
    sorted_sender = jnp.take_along_axis(sender_of, sort_order, axis=1)
    counts = jnp.sum((sender_of[:, :, None] == jnp.arange(N_GY)[None, None, :]).astype(jnp.int32), axis=1)
    first_slot = jnp.cumsum(counts, axis=1) - counts
    slot_index = jnp.arange(queue, dtype=jnp.int32)[None, :] - jnp.take_along_axis(first_slot, sorted_sender, axis=1)
    slot_key = jax.random.randint(subkeys[4], (N_GX, N_GY, OLD_SLOTS), 0, 4096) * OLD_SLOTS + jnp.arange(OLD_SLOTS, dtype=jnp.int32)
    slot_perm = jnp.argsort(slot_key, axis=2).astype(jnp.int32)
    row_index = jnp.broadcast_to(jnp.arange(N_GX, dtype=jnp.int32)[:, None], (N_GX, queue))
    final_slot = slot_perm[row_index, sorted_sender, slot_index]
    receiver = (sort_order // BOX_DEV).astype(jnp.int32)
    box_index = (sort_order % BOX_DEV).astype(jnp.int32)
    owner_table = jnp.full((N_GX, N_GY, OLD_SLOTS), N_GY, jnp.int32).at[row_index, sorted_sender, final_slot].set(receiver)
    box_table = jnp.zeros((N_GX, N_GY, OLD_SLOTS), jnp.int32).at[row_index, sorted_sender, final_slot].set(box_index)
    return (owner_table, box_table)


def draw_send_owner(key, part):
    return regrid_tables(key)[0]


def draw_send_box(key, part):
    return regrid_tables(key)[1]


def draw_rhs_old(key, part):
    key = jax.random.fold_in(key, 7)
    subkeys = jax.random.split(key, 2)
    extent = (N_GX, N_GY, OLD_SLOTS, NZ, BS * BS)
    box_extent = (N_GX, N_GY, OLD_SLOTS, 1, 1)
    rough = jax.random.normal(subkeys[0], extent, jnp.float32)
    offset = jax.random.uniform(subkeys[1], box_extent, jnp.float32, 0.5, 1.5)
    return jnp.clip(rough + offset, -6.0, 6.0)


def block_levels(stream_key, shape, cuts, smallest, largest):
    def one(position, blocks):
        draws = jax.random.uniform(jax.random.fold_in(jax.random.fold_in(stream_key, 6), position), (blocks,), jnp.float32, smallest / len(cuts), largest / len(cuts))
        return jnp.repeat(jnp.exp(draws), shape[position] // blocks).reshape((-1,) + (1,) * (len(shape) - position - 1))

    factor_of = one(*cuts[0])
    for cut in cuts[1:]:
        factor_of = factor_of * one(*cut)
    return factor_of


def setup_inputs(seed: int = 0) -> dict:
    splits = jax.random.split(jax.random.key(seed), 5)
    send_owner = draw_send_owner(jax.random.fold_in(splits[4], 71), 0)
    send_box = draw_send_box(jax.random.fold_in(splits[4], 71), 0)
    rho_old = jnp.clip(jnp.exp(math.log(1.2) - 2.0794415 * jax.random.uniform(splits[2], (N_GX, N_GY, OLD_SLOTS, NZ, BS * BS), jnp.float32) ** block_levels(splits[2], (N_GX, N_GY, OLD_SLOTS, NZ, BS * BS), ((0, 32), (1, 16)), -0.2, 0.2)), 0.15, 1.2)
    rhs_old = draw_rhs_old(jax.random.fold_in(splits[4], 71), 0)
    return {"send_owner": send_owner, "send_box": send_box, "rho_old": rho_old, "rhs_old": rhs_old}


def restrict_mean(field):
    extent = field.shape
    return field.reshape(extent[0] // 2, 2, extent[1] // 2, 2, extent[2] // 2, 2).mean(axis=(1, 3, 5))


def prolong_copy(coarse):
    extent = coarse.shape
    wide = jnp.broadcast_to(coarse[:, None, :, None, :, None], (extent[0], 2, extent[1], 2, extent[2], 2))
    return wide.reshape(2 * extent[0], 2 * extent[1], 2 * extent[2])


def face_weights(padded):
    centre = padded[1:-1, 1:-1, 1:-1]
    to_east = (centre + padded[2:, 1:-1, 1:-1]) * 0.5
    to_west = (padded[:-2, 1:-1, 1:-1] + centre) * 0.5
    to_north = (centre + padded[1:-1, 2:, 1:-1]) * 0.5
    to_south = (padded[1:-1, :-2, 1:-1] + centre) * 0.5
    to_upper = (centre + padded[1:-1, 1:-1, 2:]) * 0.5
    to_lower = (padded[1:-1, 1:-1, :-2] + centre) * 0.5
    return (to_east, to_west, to_north, to_south, to_upper, to_lower)


def neighbour_sum(padded, weights):
    summed = weights[0] * padded[2:, 1:-1, 1:-1] + weights[1] * padded[:-2, 1:-1, 1:-1]
    summed = summed + weights[2] * padded[1:-1, 2:, 1:-1] + weights[3] * padded[1:-1, :-2, 1:-1]
    summed = summed + weights[4] * padded[1:-1, 1:-1, 2:] + weights[5] * padded[1:-1, 1:-1, :-2]
    return summed


def make_level(padded, weight_scale):
    weights = face_weights(padded)
    summed = weights[0] + weights[1]
    summed = summed + weights[2] + weights[3]
    summed = summed + weights[4] + weights[5]
    return (weights, weight_scale * summed, weight_scale)


def colour_mask(extent):
    index_x = jnp.arange(extent[0], dtype=jnp.int32)
    index_y = jnp.arange(extent[1], dtype=jnp.int32)
    index_z = jnp.arange(extent[2], dtype=jnp.int32)
    return (index_x[:, None, None] + index_y[None, :, None] + index_z[None, None, :]) % 2


def smooth(field, source, level_data, pad_fn, parity):
    weights, diagonal, weight_scale = level_data
    for colour in (0, 1):
        summed = neighbour_sum(pad_fn(field), weights)
        field = jnp.where(parity == colour, (source + weight_scale * summed) / diagonal, field)
    return field


def residual_of(field, source, level_data, pad_fn):
    weights, diagonal, weight_scale = level_data
    summed = neighbour_sum(pad_fn(field), weights)
    return source - (diagonal * field - weight_scale * summed)


def pad_zero(field):
    return jnp.pad(field, 1)


def place_boxes(values, send_owner, send_box):
    row_index = jnp.arange(N_GX, dtype=jnp.int32)[:, None, None]
    target = (row_index * N_GY + send_owner) * BOX_DEV + send_box
    target = jnp.where(send_owner < N_GY, target, N_GX * N_GY * BOX_DEV).reshape(-1).astype(jnp.int32)
    box_data = jnp.zeros((N_GX * N_GY * BOX_DEV, NZ, BS * BS), jnp.float32)
    box_data = box_data.at[target].set(values.reshape(-1, NZ, BS * BS), mode="drop")
    box_data = box_data.reshape(N_GX, N_GY, CX // BS, CY // BS, NZ, BS, BS)
    return box_data.transpose(4, 0, 2, 5, 1, 3, 6).reshape(NZ, NX, NY)


def reference(send_owner, send_box, rho_old, rhs_old):
    density = place_boxes(rho_old, send_owner, send_box)
    source = place_boxes(rhs_old, send_owner, send_box)
    inverse_fine = 1.0 / density
    inverse_mid = restrict_mean(inverse_fine)
    inverse_coarse = restrict_mean(inverse_mid)
    level_fine = make_level(pad_zero(inverse_fine), 1.0)
    level_mid = make_level(pad_zero(inverse_mid), 0.25)
    level_coarse = make_level(pad_zero(inverse_coarse), 0.0625)
    parity_fine = colour_mask(inverse_fine.shape)
    parity_mid = colour_mask(inverse_mid.shape)
    parity_coarse = colour_mask(inverse_coarse.shape)
    field = jnp.zeros_like(source)
    for cycle_step in range(CYCLES):
        field = smooth(field, source, level_fine, pad_zero, parity_fine)
        source_mid = restrict_mean(residual_of(field, source, level_fine, pad_zero))
        field_mid = smooth(jnp.zeros_like(source_mid), source_mid, level_mid, pad_zero, parity_mid)
        source_coarse = restrict_mean(residual_of(field_mid, source_mid, level_mid, pad_zero))
        field_coarse = jnp.zeros_like(source_coarse)
        for sweep_step in range(BOTTOM):
            field_coarse = smooth(field_coarse, source_coarse, level_coarse, pad_zero, parity_coarse)
        field_mid = smooth(field_mid + prolong_copy(field_coarse), source_mid, level_mid, pad_zero, parity_mid)
        field = smooth(field + prolong_copy(field_mid), source, level_fine, pad_zero, parity_fine)
    return field
```

```python
import functools

import jax
import jax.numpy as jnp
from jax import lax
from jax.experimental import pallas as pl
from jax.experimental.pallas import tpu as pltpu
from jax.sharding import PartitionSpec as P

MESH = pl.DeviceIdType.MESH
F32 = jnp.float32
I32 = jnp.int32
CYCLES = 2
BOTTOM = 6
SIDE = [(dx, dy) for dx in (-2, -1, 0, 1, 2) for dy in (-1, 0, 1) if (dx, dy) != (0, 0)]


def iota(shape, dim):
    return lax.broadcasted_iota(I32, shape, dim)


def turn(x, shift, axis):
    return pltpu.roll(x, shift % x.shape[axis], axis)


def split3(x):
    high = x.astype(jnp.bfloat16).astype(F32)
    rest = x - high
    middle = rest.astype(jnp.bfloat16).astype(F32)
    return high, middle, rest - middle


def kernel(
    nx, ny, slots_ref, table_ref, rho_hbm, rhs_hbm, out_ref,
    rho_in, rhs_in, rho_out, rhs_out, rho_got, rhs_got, tables,
    beta, source, phi_a, phi_b, wx, wy, wz, inv, diag,
    strips, strips_got,
    beta1, g1, v1, wx1, wy1, wz1, inv1, diag1,
    pairs, tiles, tiles_got, spread, gather, wide,
    in_sem, send_sem, recv_sem,
):
    gx, gy = lax.axis_index("gx"), lax.axis_index("gy")
    ky = 4 if ny % 4 == 0 else ny
    kx = ny // ky

    def beside(dx, dy):
        return (lax.rem(gx + (dx + nx), nx), lax.rem(gy + (dy + ny), ny))

    def mate(o):
        return lax.rem(gy // ky + o // ky, kx) * ky + lax.rem(gy % ky + o % ky, ky)

    used = [0]

    def send(src, dst, device):
        k = used[0]
        used[0] += 1
        copy = pltpu.make_async_remote_copy(
            src_ref=src, dst_ref=dst, send_sem=send_sem.at[k], recv_sem=recv_sem.at[k],
            device_id=device, device_id_type=MESH,
        )
        copy.start()
        return copy

    loads = [
        pltpu.make_async_copy(rho_hbm, rho_in, in_sem.at[0]),
        pltpu.make_async_copy(rhs_hbm, rhs_in, in_sem.at[1]),
    ]
    for load in loads:
        load.start()

    barrier = pltpu.get_barrier_semaphore()
    peers = [(gx, mate(o)) for o in range(1, ny)] + [beside(dx, dy) for dx, dy in SIDE if dx != 0]
    for device in peers:
        pl.semaphore_signal(barrier, inc=1, device_id=device, device_id_type=MESH)
    pl.semaphore_wait(barrier, len(peers))

    order = sorted(range(1, ny), key=lambda o: (min(o // ky, kx - o // ky) + min(o % ky, ky - o % ky), o))
    table_copies = [send(table_ref, tables.at[o], (gx, mate(o))) for o in order]
    box_copies = []
    for load, held, leaving, arrived in (
        (loads[0], rho_in, rho_out, rho_got),
        (loads[1], rhs_in, rhs_out, rhs_got),
    ):
        load.wait()
        copies = []
        for o in [*order, 0]:
            d = mate(o)
            for r in range(2):
                box = held[slots_ref[2 * d + r]]
                if o == 0:
                    arrived[r] = box
                else:
                    leaving[2 * o + r] = box
            if o:
                copies.append(
                    send(leaving.at[pl.ds(2 * o, 2)], arrived.at[pl.ds(2 * o, 2)], (gx, d))
                )
        box_copies.append(copies)

    k, n = iota((128, 512), 0), iota((128, 512), 1)
    lane = n % 256
    place = jnp.where(lane < 192, lane // 4 + 16, lane // 4 - 48)
    spread[...] = jnp.where((k // 64 == n // 256) & (k % 64 == place), 1.0, 0.0).astype(jnp.bfloat16)
    k, n = iota((256, 128), 0), iota((256, 128), 1)
    lane = k % 128
    hit = (k // 128 == n // 64) & (lane % 2 == 0) & (lane // 4 + 16 == n % 64)
    gather[...] = jnp.where(hit, 0.125, 0.0).astype(jnp.bfloat16)
    nothing = jnp.zeros((8, 256), F32)
    for ref, last in ((beta, 65), (source, 65), (wx, 65), (beta1, 33), (wx1, 33)):
        ref[0] = nothing
        ref[last] = nothing
    for ref, last in ((phi_a, 61), (v1, 29)):
        ref[4] = nothing
        ref[last] = nothing

    lanes128 = iota((8, 128), 1)
    sub, lane256 = iota((8, 256), 0), iota((8, 256), 1)

    tables[0] = table_ref[...]
    for copy in table_copies:
        copy.wait()
    owners, ids = tables[:, 0, :], tables[:, 1, :]
    mine = owners == gy
    slot = iota((ny, 128), 1)
    first = jnp.min(jnp.where(mine, slot, 128), axis=1, keepdims=True)
    index = 2 * iota((ny, 128), 0) + jnp.where(slot == first, 0, 1)
    where_from = [jnp.max(jnp.where(mine & (ids == b), index, 0)) for b in range(4)]

    def assemble(arrived, field, invert):
        for g in range(8):
            parts = [arrived[where_from[b], :, 128 * g : 128 * g + 128] for b in range(4)]
            for r in range(4):
                row = parts[0] if r == 0 else turn(parts[0], -32 * r, 1)
                for b in range(1, 4):
                    moved = parts[b] if b == r else turn(parts[b], 32 * (b - r), 1)
                    row = jnp.where(lanes128 >= 32 * b, moved, row)
                if invert:
                    row = 1.0 / row
                field[17 + 4 * g + r, :, 0:128] = row

    def exchange(which, field):
        left, right = strips.at[which, 0], strips.at[which, 1]
        from_left, from_right = strips_got.at[which, 0], strips_got.at[which, 1]
        main = pl.ds(0, 128)
        copies = [
            send(field.at[pl.ds(33, 16), :, main], field.at[pl.ds(1, 16), :, main], beside(1, 0)),
            send(field.at[pl.ds(17, 16), :, main], field.at[pl.ds(49, 16), :, main], beside(-1, 0)),
        ]

        def pack(j, carry):
            low = high = None
            for q in range(8):
                row = field[17 + 8 * j + q, :, 0:128]
                a, b = turn(row, 16 * q, 1), turn(row, 16 * q - 112, 1)
                low = a if q == 0 else jnp.where(lanes128 >= 16 * q, a, low)
                high = b if q == 0 else jnp.where(lanes128 >= 16 * q, b, high)
            left[j] = low
            right[j] = high
            return carry

        lax.fori_loop(0, 4, pack, 0)
        for dy, src, dst in ((1, right, from_left), (-1, left, from_right)):
            copies.append(send(src, dst.at[pl.ds(2, 4)], beside(0, dy)))
            copies.append(send(src.at[pl.ds(2, 2)], dst.at[pl.ds(0, 2)], beside(1, dy)))
            copies.append(send(src.at[pl.ds(0, 2)], dst.at[pl.ds(6, 2)], beside(-1, dy)))
        return copies

    row_low, row_high = jnp.where(gx > 0, 1.0, 0.0), jnp.where(gx < nx - 1, 1.0, 0.0)
    lane_low, lane_high = jnp.where(gy > 0, 1.0, 0.0), jnp.where(gy < ny - 1, 1.0, 0.0)
    in_high = lanes128 < 16
    in_low = lanes128 >= 112

    def fill(which, field, edges):
        from_left, from_right = strips_got.at[which, 0], strips_got.at[which, 1]
        scale = jnp.where(in_high, lane_high, lane_low)

        def unpack(j, carry):
            a, b = from_left[j], from_right[j]
            if edges:
                row_scale = jnp.where(j < 2, row_low, jnp.where(j < 6, 1.0, row_high))
                row_scales = scale * row_scale
            for q in range(8):
                low, high = turn(a, 112 - 16 * q, 1), turn(b, -16 * q, 1)
                both = jnp.where(in_high, high, jnp.where(in_low, low, 0.0))
                e = 1 + 8 * j + q
                if edges:
                    both = both * row_scales
                    field[e, :, 0:128] = field[e, :, 0:128] * row_scale
                field[e, :, 128:256] = both
            return carry

        lax.fori_loop(0, 8, unpack, 0)

    def blocks(low, count, step, body):
        def run(i, carry):
            body(low + step * i)
            return carry

        lax.fori_loop(0, count // step, run, 0)

    def make_weights(b_ref, refs, count, step, sh, scale):
        rx, ry, rz, ri, rd = refs
        half = 0.5 * scale
        top, bottom = sub < 8 - sh, sub >= sh

        def body(e):
            rows = [b_ref[e - 1 + k] for k in range(step + 2)]
            for k in range(step):
                b = rows[k + 1]
                east = half * (b + rows[k + 2])
                west = half * (rows[k] + b)
                north = half * (b + turn(b, -sh, 1))
                above = half * (b + jnp.where(top, turn(b, -sh, 0), 0.0))
                below = half * (b + jnp.where(bottom, turn(b, sh, 0), 0.0))
                total = east + west + north + turn(north, sh, 1) + above + below
                inside = b > 0.0
                rx[e + k] = east
                ry[e + k] = north
                rz[e + k] = jnp.where(top, above, 0.0)
                rd[e + k] = total
                ri[e + k] = jnp.where(inside, 1.0 / jnp.where(inside, total, 1.0), 0.0)

        blocks(1, count, step, body)

    def neighbours(rows, k, e, refs, sh, wests):
        rx, ry, rz = refs[:3]
        v = rows[k + 1]
        east, north, up = rx[e + k], ry[e + k], rz[e + k]
        west = rx[e - 1] if k == 0 else wests[0]
        wests[0] = east
        total = east * rows[k + 2] + west * rows[k]
        total = total + north * turn(v, -sh, 1) + turn(north * v, sh, 1)
        return total + (up * turn(v, -sh, 0) + turn(up * v, sh, 0))

    def even(sh):
        return (sub // sh + lane256 // sh) % 2 == 0

    def colour_step(v_ref, g_ref, refs, colour, low, count, step, sh, store=None):
        ri = refs[3]
        mask_even = even(sh)
        mask_odd = jnp.logical_not(mask_even)

        def body(e):
            rows = [v_ref[e - 1 + k] for k in range(step + 2)]
            wests = [None]
            for k in range(step):
                new = (g_ref[e + k] + neighbours(rows, k, e, refs, sh, wests)) * ri[e + k]
                mask = mask_even if (low + k + 1 + colour) % 2 == 0 else mask_odd
                new = jnp.where(mask, new, rows[k + 1])
                if store is None:
                    v_ref[e + k] = new
                else:
                    store(e + k, new)

        blocks(low, count, step, body)

    def first_colour(v_ref, g_ref, refs, low, count, step, sh):
        ri = refs[3]
        mask_even = even(sh)
        mask_odd = jnp.logical_not(mask_even)

        def body(e):
            for k in range(step):
                mask = mask_even if (low + k + 1) % 2 == 0 else mask_odd
                v_ref[e + k] = jnp.where(mask, g_ref[e + k] * ri[e + k], 0.0)

        blocks(low, count, step, body)

    def residual_rows(v_ref, g_ref, refs, e, count, sh):
        rows = [v_ref[e - 1 + k] for k in range(count + 2)]
        wests = [None]
        out = []
        for k in range(count):
            total = neighbours(rows, k, e, refs, sh, wests)
            out.append(g_ref[e + k] - (refs[4][e + k] * rows[k + 1] - total))
        return out

    sub_even, lane_even = sub % 2 == 0, lane256 % 2 == 0

    def mean8(t):
        t = t + jnp.where(sub_even, turn(t, -1, 0), turn(t, 1, 0))
        t = t + jnp.where(lane_even, turn(t, -1, 1), turn(t, 1, 1))
        return t * 0.125

    def to_tiles(which):
        a = pairs[:, 0, :] + pairs[:, 2, :]
        b = pairs[:, 4, :] + pairs[:, 6, :]
        stack = jnp.concatenate([*split3(jnp.concatenate([a, b], axis=1)), jnp.zeros((8, 256), F32)], axis=0)
        dots = jnp.dot(stack.astype(jnp.bfloat16), gather[...], preferred_element_type=F32)
        tile = (dots[0:8] + dots[8:16]) + dots[16:24]
        tiles[which, 1] = tile
        tiles[which, 2] = turn(tile, -32, 1)
        tiles[which, 0] = turn(tile, 32, 1)
        tiles_got[which, 2, 1] = tile
        return [
            send(tiles.at[which, 1 + dy], tiles_got.at[which, 2 - dx, 1 - dy], beside(dx, dy))
            for dx, dy in SIDE
        ]

    lanes64 = lanes128 % 64

    def coarse_field(which):
        rows = [
            jnp.where(
                lanes64 < 16, tiles_got[which, g, 0],
                jnp.where(lanes64 < 48, tiles_got[which, g, 1], tiles_got[which, g, 2]),
            )
            for g in range(5)
        ]
        return jnp.concatenate(rows, axis=0)

    def wait(copies):
        for copy in copies:
            copy.wait()

    fine = (wx, wy, wz, inv, diag)
    mid = (wx1, wy1, wz1, inv1, diag1)
    wait(box_copies[0])
    assemble(rho_got, beta, True)
    wait(exchange(0, beta))
    fill(0, beta, True)

    def restrict_beta(e):
        for k in range(2):
            beta1[e + k] = mean8(beta[2 * (e + k) - 1] + beta[2 * (e + k)])

    blocks(1, 32, 2, restrict_beta)

    def pair_beta(c):
        pairs[c] = beta1[9 + 2 * c, :, 0:128] + beta1[10 + 2 * c, :, 0:128]

    blocks(0, 8, 1, pair_beta)
    tile_copies = to_tiles(0)
    make_weights(beta, fine, 64, 4, 1, 1.0)
    make_weights(beta1, mid, 32, 4, 2, 0.25)
    wait(tile_copies)
    rows40, cols40 = iota((40, 128), 0), iota((40, 128), 1) % 64
    at_x, at_y = gx * 8 + rows40 - 16, gy * 32 + cols40 - 16
    in_grid = (at_x >= 0) & (at_x < 8 * nx) & (at_y >= 0) & (at_y < 32 * ny)
    b2 = jnp.where(in_grid, coarse_field(0), 0.0)
    half = 0.5 * 0.0625
    cx = half * (b2 + turn(b2, -1, 0))
    cy = half * (b2 + turn(b2, -1, 1))
    cz = half * (b2 + turn(b2, 64, 1))
    total = cx + turn(cx, 1, 0) + cy + turn(cy, 1, 1) + cz + half * b2
    inside = b2 > 0.0
    ci = jnp.where(inside, 1.0 / jnp.where(inside, total, 1.0), 0.0)
    coarse_even = (rows40 + cols40 + iota((40, 128), 1) // 64) % 2 == 0
    coarse_weights = (cx, cy, cz, ci)
    for k in range(4):
        wide[k] = coarse_weights[k]

    wait(box_copies[1])
    assemble(rhs_got, source, False)
    wait(exchange(1, source))
    fill(1, source, False)

    for cycle in range(CYCLES):
        phi = phi_a if cycle == 0 else phi_b
        if cycle == 0:
            first_colour(phi, source, fine, 5, 56, 8, 1)
        else:
            colour_step(phi, source, fine, 0, 5, 56, 8, 1)
        colour_step(phi, source, fine, 1, 5, 56, 8, 1)

        def restrict(e):
            out = residual_rows(phi, source, fine, 2 * e - 1, 4, 1)
            for k in range(2):
                g1[e + k] = mean8(out[2 * k] + out[2 * k + 1])

        blocks(5, 24, 2, restrict)
        first_colour(v1, g1, mid, 5, 24, 8, 2)
        colour_step(v1, g1, mid, 1, 5, 24, 4, 2)

        def pair_residual(c):
            out = residual_rows(v1, g1, mid, 9 + 2 * c, 2, 2)
            pairs[c] = (out[0] + out[1])[:, 0:128]

        blocks(0, 8, 1, pair_residual)
        wait(to_tiles(1 + cycle))
        g2 = coarse_field(1 + cycle)
        cx, cy, cz, ci = wide[0], wide[1], wide[2], wide[3]
        v2 = jnp.where(coarse_even, g2 * ci, 0.0)
        for step in range(1, 2 * BOTTOM):
            total = cx * turn(v2, -1, 0) + turn(cx * v2, 1, 0)
            total = total + cy * turn(v2, -1, 1) + turn(cy * v2, 1, 1)
            total = total + cz * turn(v2, 64, 1)
            new = (g2 + total) * ci
            v2 = jnp.where(coarse_even, new, v2) if step % 2 == 0 else jnp.where(coarse_even, v2, new)
        stack = jnp.concatenate(split3(v2[8:40]), axis=0)
        dots = jnp.dot(stack.astype(jnp.bfloat16), spread[...], preferred_element_type=F32)
        grown = (dots[0:32] + dots[32:64]) + dots[64:96]
        for c in range(1, 13):
            row = grown[c + 5 : c + 6]
            extra = jnp.where(sub < 4, row[:, 0:256], row[:, 256:512])
            for k in range(2):
                v1[3 + 2 * c + k] = v1[3 + 2 * c + k] + extra
        colour_step(v1, g1, mid, 0, 5, 24, 4, 2)
        colour_step(v1, g1, mid, 1, 5, 24, 4, 2)

        def prolong(e):
            for k in range(2):
                extra = v1[e + k]
                for row in (2 * (e + k) - 1, 2 * (e + k)):
                    phi[row] = phi[row] + extra

        blocks(7, 20, 2, prolong)
        colour_step(phi, source, fine, 0, 13, 40, 8, 1)
        if cycle < CYCLES - 1:

            def keep(e, value):
                phi_b[e] = value

            colour_step(phi, source, fine, 1, 17, 32, 8, 1, keep)
            wait(exchange(2, phi_b))
            fill(2, phi_b, True)
        else:

            def give(e, value):
                out_ref[e - 17] = value[:, 0:128]

            colour_step(phi, source, fine, 1, 17, 32, 8, 1, give)


def local(nx, ny, send_owner, send_box, rho_old, rhs_old):
    slots = send_owner.shape[2]
    owner, box = send_owner.reshape(slots), send_box.reshape(slots)
    match = owner[None, :] == jnp.arange(ny, dtype=I32)[:, None]
    place = jnp.arange(slots, dtype=I32)[None, :]
    first = jnp.min(jnp.where(match, place, slots - 1), axis=1)
    last = jnp.max(jnp.where(match, place, 0), axis=1)
    pick = jnp.stack([first, last], axis=1).reshape(2 * ny)
    table = jnp.pad(jnp.stack([owner, box]), ((0, 6), (0, 128 - slots)), constant_values=-1)
    depth, cells = rho_old.shape[3:]
    copies = 3 * (ny - 1) + 3 * 8 + 3 * len(SIDE)

    def vmem(*shape):
        return pltpu.VMEM(shape, F32)

    boxes = vmem(2 * ny, 8, 1024)
    scratch = [
        vmem(slots, 8, 1024), vmem(slots, 8, 1024), boxes, boxes, boxes, boxes, pltpu.VMEM((ny, 8, 128), I32),
        *[vmem(66, 8, 256)] * 9,
        vmem(3, 2, 4, 8, 128), vmem(3, 2, 8, 8, 128),
        *[vmem(34, 8, 256)] * 8,
        vmem(8, 8, 128), vmem(3, 3, 8, 128), vmem(3, 5, 3, 8, 128),
        pltpu.VMEM((128, 512), jnp.bfloat16), pltpu.VMEM((256, 128), jnp.bfloat16), vmem(4, 40, 128),
        pltpu.SemaphoreType.DMA((2,)), pltpu.SemaphoreType.DMA((copies,)), pltpu.SemaphoreType.DMA((copies,)),
    ]
    out = pl.pallas_call(
        functools.partial(kernel, nx, ny),
        out_shape=jax.ShapeDtypeStruct((32, 8, 128), F32),
        in_specs=[
            pl.BlockSpec(memory_space=pltpu.SMEM),
            pl.BlockSpec(memory_space=pltpu.VMEM),
            pl.BlockSpec(memory_space=pl.ANY),
            pl.BlockSpec(memory_space=pl.ANY),
        ],
        out_specs=pl.BlockSpec(memory_space=pltpu.VMEM),
        scratch_shapes=scratch,
        compiler_params=pltpu.CompilerParams(
            collective_id=0, has_side_effects=True, vmem_limit_bytes=40 * 1024 * 1024
        ),
        name="regrid_cycles",
    )(pick, table, rho_old.reshape(slots, depth, cells), rhs_old.reshape(slots, depth, cells))
    return out.transpose(1, 0, 2)


def solution(mesh):
    placed = (
        P("gx", "gy", None),
        P("gx", "gy", None),
        P("gx", "gy", None, None, None),
        P("gx", "gy", None, None, None),
    )
    return jax.shard_map(
        functools.partial(local, mesh.shape["gx"], mesh.shape["gy"]),
        mesh=mesh, in_specs=placed, out_specs=P(None, "gx", "gy"), check_vma=False,
    )
```

```python
import functools

import jax
import jax.numpy as jnp
from jax import lax
from jax.experimental import pallas as pl
from jax.experimental.pallas import tpu as pltpu
from jax.sharding import PartitionSpec as P

MESH = pl.DeviceIdType.MESH
F32 = jnp.float32
I32 = jnp.int32
CYCLES = 2
BOTTOM = 6
SIDE = [(dx, dy) for dx in (-2, -1, 0, 1, 2) for dy in (-1, 0, 1) if (dx, dy) != (0, 0)]


def iota(shape, dim):
    return lax.broadcasted_iota(I32, shape, dim)


def turn(x, shift, axis):
    return pltpu.roll(x, shift % x.shape[axis], axis)


def split3(x):
    high = x.astype(jnp.bfloat16).astype(F32)
    rest = x - high
    middle = rest.astype(jnp.bfloat16).astype(F32)
    return high, middle, rest - middle


def kernel(
    nx, ny, slots_ref, table_ref, rho_hbm, rhs_hbm, out_ref,
    rho_in, rhs_in, rho_out, rhs_out, rho_got, rhs_got, tables,
    beta, source, phi_a, phi_b, wx, wy, wz, inv, diag,
    strips, strips_got,
    beta1, g1, v1, wx1, wy1, wz1, inv1, diag1,
    pairs, tiles, tiles_got, spread, gather, wide,
    in_sem, send_sem, recv_sem,
):
    gx, gy = lax.axis_index("gx"), lax.axis_index("gy")
    ky = 4 if ny % 4 == 0 else ny
    kx = ny // ky

    def beside(dx, dy):
        return (lax.rem(gx + (dx + nx), nx), lax.rem(gy + (dy + ny), ny))

    def mate(o):
        return lax.rem(gy // ky + o // ky, kx) * ky + lax.rem(gy % ky + o % ky, ky)

    used = [0]

    def send(src, dst, device):
        k = used[0]
        used[0] += 1
        copy = pltpu.make_async_remote_copy(
            src_ref=src, dst_ref=dst, send_sem=send_sem.at[k], recv_sem=recv_sem.at[k],
            device_id=device, device_id_type=MESH,
        )
        copy.start()
        return copy

    loads = [
        pltpu.make_async_copy(rho_hbm, rho_in, in_sem.at[0]),
        pltpu.make_async_copy(rhs_hbm, rhs_in, in_sem.at[1]),
    ]
    for load in loads:
        load.start()

    barrier = pltpu.get_barrier_semaphore()
    peers = [(gx, mate(o)) for o in range(1, ny)] + [beside(dx, dy) for dx, dy in SIDE if dx != 0]
    for device in peers:
        pl.semaphore_signal(barrier, inc=1, device_id=device, device_id_type=MESH)
    pl.semaphore_wait(barrier, len(peers))

    order = sorted(range(1, ny), key=lambda o: (min(o // ky, kx - o // ky) + min(o % ky, ky - o % ky), o))
    table_copies = [send(table_ref, tables.at[o], (gx, mate(o))) for o in order]
    box_copies = []
    for load, held, leaving, arrived in (
        (loads[0], rho_in, rho_out, rho_got),
        (loads[1], rhs_in, rhs_out, rhs_got),
    ):
        load.wait()
        copies = []
        for o in [*order, 0]:
            d = mate(o)
            for r in range(2):
                box = held[slots_ref[2 * d + r]]
                if o == 0:
                    arrived[r] = box
                else:
                    leaving[2 * o + r] = box
            if o:
                copies.append(
                    send(leaving.at[pl.ds(2 * o, 2)], arrived.at[pl.ds(2 * o, 2)], (gx, d))
                )
        box_copies.append(copies)

    k, n = iota((128, 512), 0), iota((128, 512), 1)
    lane = n % 256
    place = jnp.where(lane < 192, lane // 4 + 16, lane // 4 - 48)
    spread[...] = jnp.where((k // 64 == n // 256) & (k % 64 == place), 1.0, 0.0).astype(jnp.bfloat16)
    k, n = iota((256, 128), 0), iota((256, 128), 1)
    lane = k % 128
    hit = (k // 128 == n // 64) & (lane % 2 == 0) & (lane // 4 + 16 == n % 64)
    gather[...] = jnp.where(hit, 0.125, 0.0).astype(jnp.bfloat16)
    nothing = jnp.zeros((8, 256), F32)
    for ref, last in ((beta, 65), (source, 65), (wx, 65), (beta1, 33), (wx1, 33)):
        ref[0] = nothing
        ref[last] = nothing
    for ref, last in ((phi_a, 61), (v1, 29)):
        ref[4] = nothing
        ref[last] = nothing

    lanes128 = iota((8, 128), 1)
    sub, lane256 = iota((8, 256), 0), iota((8, 256), 1)

    tables[0] = table_ref[...]
    for copy in table_copies:
        copy.wait()
    owners, ids = tables[:, 0, :], tables[:, 1, :]
    mine = owners == gy
    slot = iota((ny, 128), 1)
    first = jnp.min(jnp.where(mine, slot, 128), axis=1, keepdims=True)
    index = 2 * iota((ny, 128), 0) + jnp.where(slot == first, 0, 1)
    where_from = [jnp.max(jnp.where(mine & (ids == b), index, 0)) for b in range(4)]

    def assemble(arrived, field, invert):
        for g in range(8):
            parts = [arrived[where_from[b], :, 128 * g : 128 * g + 128] for b in range(4)]
            for r in range(4):
                row = parts[0] if r == 0 else turn(parts[0], -32 * r, 1)
                for b in range(1, 4):
                    moved = parts[b] if b == r else turn(parts[b], 32 * (b - r), 1)
                    row = jnp.where(lanes128 >= 32 * b, moved, row)
                if invert:
                    row = 1.0 / row
                field[17 + 4 * g + r, :, 0:128] = row

    def exchange(which, field):
        left, right = strips.at[which, 0], strips.at[which, 1]
        from_left, from_right = strips_got.at[which, 0], strips_got.at[which, 1]
        main = pl.ds(0, 128)
        copies = [
            send(field.at[pl.ds(33, 16), :, main], field.at[pl.ds(1, 16), :, main], beside(1, 0)),
            send(field.at[pl.ds(17, 16), :, main], field.at[pl.ds(49, 16), :, main], beside(-1, 0)),
        ]

        def pack(j, carry):
            low = high = None
            for q in range(8):
                row = field[17 + 8 * j + q, :, 0:128]
                a, b = turn(row, 16 * q, 1), turn(row, 16 * q - 112, 1)
                low = a if q == 0 else jnp.where(lanes128 >= 16 * q, a, low)
                high = b if q == 0 else jnp.where(lanes128 >= 16 * q, b, high)
            left[j] = low
            right[j] = high
            return carry

        lax.fori_loop(0, 4, pack, 0)
        for dy, src, dst in ((1, right, from_left), (-1, left, from_right)):
            copies.append(send(src, dst.at[pl.ds(2, 4)], beside(0, dy)))
            copies.append(send(src.at[pl.ds(2, 2)], dst.at[pl.ds(0, 2)], beside(1, dy)))
            copies.append(send(src.at[pl.ds(0, 2)], dst.at[pl.ds(6, 2)], beside(-1, dy)))
        return copies

    row_low, row_high = jnp.where(gx > 0, 1.0, 0.0), jnp.where(gx < nx - 1, 1.0, 0.0)
    lane_low, lane_high = jnp.where(gy > 0, 1.0, 0.0), jnp.where(gy < ny - 1, 1.0, 0.0)
    in_high = lanes128 < 16
    in_low = lanes128 >= 112

    def fill(which, field, edges):
        from_left, from_right = strips_got.at[which, 0], strips_got.at[which, 1]
        scale = jnp.where(in_high, lane_high, lane_low)

        def unpack(j, carry):
            a, b = from_left[j], from_right[j]
            if edges:
                row_scale = jnp.where(j < 2, row_low, jnp.where(j < 6, 1.0, row_high))
                row_scales = scale * row_scale
            for q in range(8):
                low, high = turn(a, 112 - 16 * q, 1), turn(b, -16 * q, 1)
                both = jnp.where(in_high, high, jnp.where(in_low, low, 0.0))
                e = 1 + 8 * j + q
                if edges:
                    both = both * row_scales
                    field[e, :, 0:128] = field[e, :, 0:128] * row_scale
                field[e, :, 128:256] = both
            return carry

        lax.fori_loop(0, 8, unpack, 0)

    def blocks(low, count, step, body):
        def run(i, carry):
            body(low + step * i)
            return carry

        lax.fori_loop(0, count // step, run, 0, unroll=True)

    def make_weights(b_ref, refs, count, step, sh, scale):
        rx, ry, rz, ri, rd = refs
        half = 0.5 * scale
        top, bottom = sub < 8 - sh, sub >= sh

        def body(e):
            rows = [b_ref[e - 1 + k] for k in range(step + 2)]
            for k in range(step):
                b = rows[k + 1]
                east = half * (b + rows[k + 2])
                west = half * (rows[k] + b)
                north = half * (b + turn(b, -sh, 1))
                above = half * (b + jnp.where(top, turn(b, -sh, 0), 0.0))
                below = half * (b + jnp.where(bottom, turn(b, sh, 0), 0.0))
                total = east + west + north + turn(north, sh, 1) + above + below
                inside = b > 0.0
                rx[e + k] = east
                ry[e + k] = north
                rz[e + k] = jnp.where(top, above, 0.0)
                rd[e + k] = total
                ri[e + k] = jnp.where(inside, 1.0 / jnp.where(inside, total, 1.0), 0.0)

        blocks(1, count, step, body)

    def neighbours(rows, k, e, refs, sh, wests):
        rx, ry, rz = refs[:3]
        v = rows[k + 1]
        east, north, up = rx[e + k], ry[e + k], rz[e + k]
        west = rx[e - 1] if k == 0 else wests[0]
        wests[0] = east
        total = east * rows[k + 2] + west * rows[k]
        total = total + north * turn(v, -sh, 1) + turn(north * v, sh, 1)
        return total + (up * turn(v, -sh, 0) + turn(up * v, sh, 0))

    def even(sh):
        return (sub // sh + lane256 // sh) % 2 == 0

    def colour_step(v_ref, g_ref, refs, colour, low, count, step, sh, store=None):
        ri = refs[3]
        mask_even = even(sh)
        mask_odd = jnp.logical_not(mask_even)

        def body(e):
            rows = [v_ref[e - 1 + k] for k in range(step + 2)]
            wests = [None]
            for k in range(step):
                new = (g_ref[e + k] + neighbours(rows, k, e, refs, sh, wests)) * ri[e + k]
                mask = mask_even if (low + k + 1 + colour) % 2 == 0 else mask_odd
                new = jnp.where(mask, new, rows[k + 1])
                if store is None:
                    v_ref[e + k] = new
                else:
                    store(e + k, new)

        blocks(low, count, step, body)

    def first_colour(v_ref, g_ref, refs, low, count, step, sh):
        ri = refs[3]
        mask_even = even(sh)
        mask_odd = jnp.logical_not(mask_even)

        def body(e):
            for k in range(step):
                mask = mask_even if (low + k + 1) % 2 == 0 else mask_odd
                v_ref[e + k] = jnp.where(mask, g_ref[e + k] * ri[e + k], 0.0)

        blocks(low, count, step, body)

    def residual_rows(v_ref, g_ref, refs, e, count, sh):
        rows = [v_ref[e - 1 + k] for k in range(count + 2)]
        wests = [None]
        out = []
        for k in range(count):
            total = neighbours(rows, k, e, refs, sh, wests)
            out.append(g_ref[e + k] - (refs[4][e + k] * rows[k + 1] - total))
        return out

    sub_even, lane_even = sub % 2 == 0, lane256 % 2 == 0

    def mean8(t):
        t = t + jnp.where(sub_even, turn(t, -1, 0), turn(t, 1, 0))
        t = t + jnp.where(lane_even, turn(t, -1, 1), turn(t, 1, 1))
        return t * 0.125

    def to_tiles(which):
        a = pairs[:, 0, :] + pairs[:, 2, :]
        b = pairs[:, 4, :] + pairs[:, 6, :]
        stack = jnp.concatenate([*split3(jnp.concatenate([a, b], axis=1)), jnp.zeros((8, 256), F32)], axis=0)
        dots = jnp.dot(stack.astype(jnp.bfloat16), gather[...], preferred_element_type=F32)
        tile = (dots[0:8] + dots[8:16]) + dots[16:24]
        tiles[which, 1] = tile
        tiles[which, 2] = turn(tile, -32, 1)
        tiles[which, 0] = turn(tile, 32, 1)
        tiles_got[which, 2, 1] = tile
        return [
            send(tiles.at[which, 1 + dy], tiles_got.at[which, 2 - dx, 1 - dy], beside(dx, dy))
            for dx, dy in SIDE
        ]

    lanes64 = lanes128 % 64

    def coarse_field(which):
        rows = [
            jnp.where(
                lanes64 < 16, tiles_got[which, g, 0],
                jnp.where(lanes64 < 48, tiles_got[which, g, 1], tiles_got[which, g, 2]),
            )
            for g in range(5)
        ]
        return jnp.concatenate(rows, axis=0)

    def wait(copies):
        for copy in copies:
            copy.wait()

    fine = (wx, wy, wz, inv, diag)
    mid = (wx1, wy1, wz1, inv1, diag1)
    wait(box_copies[0])
    assemble(rho_got, beta, True)
    wait(exchange(0, beta))
    fill(0, beta, True)

    def restrict_beta(e):
        for k in range(2):
            beta1[e + k] = mean8(beta[2 * (e + k) - 1] + beta[2 * (e + k)])

    blocks(1, 32, 2, restrict_beta)

    def pair_beta(c):
        pairs[c] = beta1[9 + 2 * c, :, 0:128] + beta1[10 + 2 * c, :, 0:128]

    blocks(0, 8, 1, pair_beta)
    tile_copies = to_tiles(0)
    make_weights(beta, fine, 64, 4, 1, 1.0)
    make_weights(beta1, mid, 32, 4, 2, 0.25)
    wait(tile_copies)
    rows40, cols40 = iota((40, 128), 0), iota((40, 128), 1) % 64
    at_x, at_y = gx * 8 + rows40 - 16, gy * 32 + cols40 - 16
    in_grid = (at_x >= 0) & (at_x < 8 * nx) & (at_y >= 0) & (at_y < 32 * ny)
    b2 = jnp.where(in_grid, coarse_field(0), 0.0)
    half = 0.5 * 0.0625
    cx = half * (b2 + turn(b2, -1, 0))
    cy = half * (b2 + turn(b2, -1, 1))
    cz = half * (b2 + turn(b2, 64, 1))
    total = cx + turn(cx, 1, 0) + cy + turn(cy, 1, 1) + cz + half * b2
    inside = b2 > 0.0
    ci = jnp.where(inside, 1.0 / jnp.where(inside, total, 1.0), 0.0)
    coarse_even = (rows40 + cols40 + iota((40, 128), 1) // 64) % 2 == 0
    coarse_weights = (cx, cy, cz, ci)
    for k in range(4):
        wide[k] = coarse_weights[k]

    wait(box_copies[1])
    assemble(rhs_got, source, False)
    wait(exchange(1, source))
    fill(1, source, False)

    for cycle in range(CYCLES):
        phi = phi_a if cycle == 0 else phi_b
        if cycle == 0:
            first_colour(phi, source, fine, 5, 56, 8, 1)
        else:
            colour_step(phi, source, fine, 0, 5, 56, 8, 1)
        colour_step(phi, source, fine, 1, 5, 56, 8, 1)

        def restrict(e):
            out = residual_rows(phi, source, fine, 2 * e - 1, 4, 1)
            for k in range(2):
                g1[e + k] = mean8(out[2 * k] + out[2 * k + 1])

        blocks(5, 24, 2, restrict)
        first_colour(v1, g1, mid, 5, 24, 8, 2)
        colour_step(v1, g1, mid, 1, 5, 24, 4, 2)

        def pair_residual(c):
            out = residual_rows(v1, g1, mid, 9 + 2 * c, 2, 2)
            pairs[c] = (out[0] + out[1])[:, 0:128]

        blocks(0, 8, 1, pair_residual)
        wait(to_tiles(1 + cycle))
        g2 = coarse_field(1 + cycle)
        cx, cy, cz, ci = wide[0], wide[1], wide[2], wide[3]
        v2 = jnp.where(coarse_even, g2 * ci, 0.0)
        for step in range(1, 2 * BOTTOM):
            total = cx * turn(v2, -1, 0) + turn(cx * v2, 1, 0)
            total = total + cy * turn(v2, -1, 1) + turn(cy * v2, 1, 1)
            total = total + cz * turn(v2, 64, 1)
            new = (g2 + total) * ci
            v2 = jnp.where(coarse_even, new, v2) if step % 2 == 0 else jnp.where(coarse_even, v2, new)
        stack = jnp.concatenate(split3(v2[8:40]), axis=0)
        dots = jnp.dot(stack.astype(jnp.bfloat16), spread[...], preferred_element_type=F32)
        grown = (dots[0:32] + dots[32:64]) + dots[64:96]
        for c in range(1, 13):
            row = grown[c + 5 : c + 6]
            extra = jnp.where(sub < 4, row[:, 0:256], row[:, 256:512])
            for k in range(2):
                v1[3 + 2 * c + k] = v1[3 + 2 * c + k] + extra
        colour_step(v1, g1, mid, 0, 5, 24, 4, 2)
        colour_step(v1, g1, mid, 1, 5, 24, 4, 2)

        def prolong(e):
            for k in range(2):
                extra = v1[e + k]
                for row in (2 * (e + k) - 1, 2 * (e + k)):
                    phi[row] = phi[row] + extra

        blocks(7, 20, 2, prolong)
        colour_step(phi, source, fine, 0, 13, 40, 8, 1)
        if cycle < CYCLES - 1:

            def keep(e, value):
                phi_b[e] = value

            colour_step(phi, source, fine, 1, 17, 32, 8, 1, keep)
            wait(exchange(2, phi_b))
            fill(2, phi_b, True)
        else:

            def give(e, value):
                out_ref[e - 17] = value[:, 0:128]

            colour_step(phi, source, fine, 1, 17, 32, 8, 1, give)


def local(nx, ny, send_owner, send_box, rho_old, rhs_old):
    slots = send_owner.shape[2]
    owner, box = send_owner.reshape(slots), send_box.reshape(slots)
    match = owner[None, :] == jnp.arange(ny, dtype=I32)[:, None]
    place = jnp.arange(slots, dtype=I32)[None, :]
    first = jnp.min(jnp.where(match, place, slots - 1), axis=1)
    last = jnp.max(jnp.where(match, place, 0), axis=1)
    pick = jnp.stack([first, last], axis=1).reshape(2 * ny)
    table = jnp.pad(jnp.stack([owner, box]), ((0, 6), (0, 128 - slots)), constant_values=-1)
    depth, cells = rho_old.shape[3:]
    copies = 3 * (ny - 1) + 3 * 8 + 3 * len(SIDE)

    def vmem(*shape):
        return pltpu.VMEM(shape, F32)

    boxes = vmem(2 * ny, 8, 1024)
    scratch = [
        vmem(slots, 8, 1024), vmem(slots, 8, 1024), boxes, boxes, boxes, boxes, pltpu.VMEM((ny, 8, 128), I32),
        *[vmem(66, 8, 256)] * 9,
        vmem(3, 2, 4, 8, 128), vmem(3, 2, 8, 8, 128),
        *[vmem(34, 8, 256)] * 8,
        vmem(8, 8, 128), vmem(3, 3, 8, 128), vmem(3, 5, 3, 8, 128),
        pltpu.VMEM((128, 512), jnp.bfloat16), pltpu.VMEM((256, 128), jnp.bfloat16), vmem(4, 40, 128),
        pltpu.SemaphoreType.DMA((2,)), pltpu.SemaphoreType.DMA((copies,)), pltpu.SemaphoreType.DMA((copies,)),
    ]
    out = pl.pallas_call(
        functools.partial(kernel, nx, ny),
        out_shape=jax.ShapeDtypeStruct((32, 8, 128), F32),
        in_specs=[
            pl.BlockSpec(memory_space=pltpu.SMEM),
            pl.BlockSpec(memory_space=pltpu.VMEM),
            pl.BlockSpec(memory_space=pl.ANY),
            pl.BlockSpec(memory_space=pl.ANY),
        ],
        out_specs=pl.BlockSpec(memory_space=pltpu.VMEM),
        scratch_shapes=scratch,
        compiler_params=pltpu.CompilerParams(
            collective_id=0, has_side_effects=True, vmem_limit_bytes=60 * 1024 * 1024
        ),
        name="regrid_cycles",
    )(pick, table, rho_old.reshape(slots, depth, cells), rhs_old.reshape(slots, depth, cells))
    return out.transpose(1, 0, 2)


def solution(mesh):
    placed = (
        P("gx", "gy", None),
        P("gx", "gy", None),
        P("gx", "gy", None, None, None),
        P("gx", "gy", None, None, None),
    )
    return jax.shard_map(
        functools.partial(local, mesh.shape["gx"], mesh.shape["gy"]),
        mesh=mesh, in_specs=placed, out_specs=P(None, "gx", "gy"), check_vma=False,
    )
```

```python
import functools

import jax
import jax.numpy as jnp
from jax import lax
from jax.experimental import pallas as pl
from jax.experimental.pallas import tpu as pltpu
from jax.sharding import PartitionSpec as P

MESH = pl.DeviceIdType.MESH
F32 = jnp.float32
I32 = jnp.int32
CYCLES = 2
BOTTOM = 6
SIDE = [(dx, dy) for dx in (-2, -1, 0, 1, 2) for dy in (-1, 0, 1) if (dx, dy) != (0, 0)]


def iota(shape, dim):
    return lax.broadcasted_iota(I32, shape, dim)


def turn(x, shift, axis):
    return pltpu.roll(x, shift % x.shape[axis], axis)


def split3(x):
    high = x.astype(jnp.bfloat16).astype(F32)
    rest = x - high
    middle = rest.astype(jnp.bfloat16).astype(F32)
    return high, middle, rest - middle


def kernel(
    nx, ny, owner_hbm, box_hbm, rho_hbm, rhs_hbm, out_ref,
    owner_in, box_in, table_ref, rho_in, rhs_in, rho_out, rhs_out, rho_got, rhs_got, tables,
    beta, source, phi, wx, wy, wz, inv, diag,
    strips, strips_got,
    beta1, g1, v1, wx1, wy1, wz1, inv1, diag1,
    pairs, tiles, tiles_got, spread, gather, wide,
    in_sem, send_sem, recv_sem,
):
    gx, gy = lax.axis_index("gx"), lax.axis_index("gy")
    ky = 4 if ny % 4 == 0 else ny
    kx = ny // ky

    def beside(dx, dy):
        return (lax.rem(gx + (dx + nx), nx), lax.rem(gy + (dy + ny), ny))

    def mate(o):
        return lax.rem(gy // ky + o // ky, kx) * ky + lax.rem(gy % ky + o % ky, ky)

    used = [0]

    def send(src, dst, device):
        k = used[0]
        used[0] += 1
        copy = pltpu.make_async_remote_copy(
            src_ref=src, dst_ref=dst, send_sem=send_sem.at[k], recv_sem=recv_sem.at[k],
            device_id=device, device_id_type=MESH,
        )
        copy.start()
        return copy

    loads = [
        pltpu.make_async_copy(rho_hbm, rho_in, in_sem.at[0]),
        pltpu.make_async_copy(rhs_hbm, rhs_in, in_sem.at[1]),
        pltpu.make_async_copy(owner_hbm, owner_in, in_sem.at[2]),
        pltpu.make_async_copy(box_hbm, box_in, in_sem.at[3]),
    ]
    for load in loads:
        load.start()

    barrier = pltpu.get_barrier_semaphore()
    peers = [(gx, mate(o)) for o in range(1, ny)] + [beside(dx, dy) for dx, dy in SIDE if dx != 0]
    for device in peers:
        pl.semaphore_signal(barrier, inc=1, device_id=device, device_id_type=MESH)
    slots = owner_in.shape[2]
    table_ref[...] = jnp.full((8, 128), -1, I32)
    loads[2].wait()
    loads[3].wait()
    owner_row = owner_in[0]
    table_ref[0:1, 0:slots] = owner_row
    table_ref[1:2, 0:slots] = box_in[0]
    at_slot = iota((1, slots), 1)
    chosen = []
    for o in range(ny):
        hit = owner_row == mate(o)
        chosen.append((jnp.min(jnp.where(hit, at_slot, slots - 1)), jnp.max(jnp.where(hit, at_slot, 0))))
    pl.semaphore_wait(barrier, len(peers))

    order = sorted(range(1, ny), key=lambda o: (min(o // ky, kx - o // ky) + min(o % ky, ky - o % ky), o))
    table_copies = [send(table_ref, tables.at[o], (gx, mate(o))) for o in order]
    box_copies = []
    for load, held, leaving, arrived in (
        (loads[0], rho_in, rho_out, rho_got),
        (loads[1], rhs_in, rhs_out, rhs_got),
    ):
        load.wait()
        copies = []
        for o in [*order, 0]:
            d = mate(o)
            for r in range(2):
                box = held[chosen[o][r]]
                if o == 0:
                    arrived[r] = box
                else:
                    leaving[2 * o + r] = box
            if o:
                copies.append(
                    send(leaving.at[pl.ds(2 * o, 2)], arrived.at[pl.ds(2 * o, 2)], (gx, d))
                )
        box_copies.append(copies)

    k, n = iota((128, 512), 0), iota((128, 512), 1)
    lane = n % 256
    place = jnp.where(lane < 192, lane // 4 + 16, lane // 4 - 48)
    spread[...] = jnp.where((k // 64 == n // 256) & (k % 64 == place), 1.0, 0.0).astype(jnp.bfloat16)
    k, n = iota((256, 128), 0), iota((256, 128), 1)
    lane = k % 128
    hit = (k // 128 == n // 64) & (lane % 2 == 0) & (lane // 4 + 16 == n % 64)
    gather[...] = jnp.where(hit, 0.125, 0.0).astype(jnp.bfloat16)
    nothing = jnp.zeros((8, 256), F32)
    for ref, last in ((beta, 81), (beta1, 41)):
        ref[0] = nothing
        ref[last] = nothing

    lanes128 = iota((8, 128), 1)
    sub, lane256 = iota((8, 256), 0), iota((8, 256), 1)

    tables[0] = table_ref[...]
    for copy in table_copies:
        copy.wait()
    owners, ids = tables[:, 0, :], tables[:, 1, :]
    mine = owners == gy
    slot = iota((ny, 128), 1)
    first = jnp.min(jnp.where(mine, slot, 128), axis=1, keepdims=True)
    index = 2 * iota((ny, 128), 0) + jnp.where(slot == first, 0, 1)
    where_from = [jnp.max(jnp.where(mine & (ids == b), index, 0)) for b in range(4)]

    def assemble(arrived, field, invert):
        for g in range(8):
            parts = [arrived[where_from[b], :, 128 * g : 128 * g + 128] for b in range(4)]
            for r in range(4):
                row = parts[0] if r == 0 else turn(parts[0], -32 * r, 1)
                for b in range(1, 4):
                    moved = parts[b] if b == r else turn(parts[b], 32 * (b - r), 1)
                    row = jnp.where(lanes128 >= 32 * b, moved, row)
                if invert:
                    row = 1.0 / row
                field[25 + 4 * g + r, :, 0:128] = row

    def exchange(which, field):
        left, right = strips.at[which, 0], strips.at[which, 1]
        from_left, from_right = strips_got.at[which, 0], strips_got.at[which, 1]
        main = pl.ds(0, 128)
        copies = [
            send(field.at[pl.ds(33, 24), :, main], field.at[pl.ds(1, 24), :, main], beside(1, 0)),
            send(field.at[pl.ds(25, 24), :, main], field.at[pl.ds(57, 24), :, main], beside(-1, 0)),
        ]
        for j in range(8):
            low = high = None
            for q in range(4):
                row = field[25 + 4 * j + q, :, 0:128]
                a, b = turn(row, 32 * q, 1), turn(row, 32 * q - 96, 1)
                low = a if q == 0 else jnp.where(lanes128 >= 32 * q, a, low)
                high = b if q == 0 else jnp.where(lanes128 >= 32 * q, b, high)
            left[j] = low
            right[j] = high
        for dy, src, dst in ((1, right, from_left), (-1, left, from_right)):
            copies.append(send(src.at[pl.ds(2, 6)], dst.at[pl.ds(0, 6)], beside(1, dy)))
            copies.append(send(src.at[pl.ds(0, 6)], dst.at[pl.ds(14, 6)], beside(-1, dy)))
            copies.append(send(src, dst.at[pl.ds(6, 8)], beside(0, dy)))
        return copies

    row_low, row_high = jnp.where(gx > 0, 1.0, 0.0), jnp.where(gx < nx - 1, 1.0, 0.0)
    lane_low, lane_high = jnp.where(gy > 0, 1.0, 0.0), jnp.where(gy < ny - 1, 1.0, 0.0)
    in_high = lanes128 < 32
    in_low = lanes128 >= 96

    def fill(which, field, edges):
        from_left, from_right = strips_got.at[which, 0], strips_got.at[which, 1]
        scale = jnp.where(in_high, lane_high, lane_low)

        for j in range(20):
            a, b = from_left[j], from_right[j]
            row_scale = row_low if j < 6 else row_high if j >= 14 else 1.0
            for q in range(4):
                low, high = turn(a, 96 - 32 * q, 1), turn(b, -32 * q, 1)
                both = jnp.where(in_high, high, jnp.where(in_low, low, 0.0))
                e = 1 + 4 * j + q
                if edges:
                    both = both * (scale * row_scale)
                    if not 6 <= j < 14:
                        field[e, :, 0:128] = field[e, :, 0:128] * row_scale
                field[e, :, 128:256] = both

    def blocks(low, count, step, body):
        for e in range(low, low + count, step):
            body(e, min(step, low + count - e))

    def make_weights(b_ref, refs, count, step, sh, scale):
        rx, ry, rz, ri, rd = refs
        half = 0.5 * scale
        top, bottom = sub < 8 - sh, sub >= sh

        def body(e, step):
            rows = [b_ref[e - 1 + k] for k in range(step + 2)]
            for k in range(step):
                b = rows[k + 1]
                east = half * (b + rows[k + 2])
                west = half * (rows[k] + b)
                north = half * (b + turn(b, -sh, 1))
                above = half * (b + jnp.where(top, turn(b, -sh, 0), 0.0))
                below = half * (b + jnp.where(bottom, turn(b, sh, 0), 0.0))
                total = east + west + north + turn(north, sh, 1) + above + below
                inside = b > 0.0
                rx[e + k] = east
                ry[e + k] = north
                rz[e + k] = jnp.where(top, above, 0.0)
                rd[e + k] = total
                ri[e + k] = jnp.where(inside, 1.0 / jnp.where(inside, total, 1.0), 0.0)

        blocks(1, count, step, body)

    def neighbours(rows, k, e, refs, sh, wests):
        rx, ry, rz = refs[:3]
        v = rows[k + 1]
        east, north, up = rx[e + k], ry[e + k], rz[e + k]
        west = rx[e - 1] if k == 0 else wests[0]
        wests[0] = east
        total = east * rows[k + 2] + west * rows[k]
        total = total + north * turn(v, -sh, 1) + turn(north * v, sh, 1)
        return total + (up * turn(v, -sh, 0) + turn(up * v, sh, 0))

    def even(sh):
        return (sub // sh + lane256 // sh) % 2 == 0

    def colour_step(v_ref, g_ref, refs, colour, low, count, step, sh, store=None):
        ri = refs[3]
        mask_even = even(sh)
        mask_odd = jnp.logical_not(mask_even)

        def body(e, step):
            rows = [v_ref[e - 1 + k] for k in range(step + 2)]
            wests = [None]
            for k in range(step):
                new = (g_ref[e + k] + neighbours(rows, k, e, refs, sh, wests)) * ri[e + k]
                mask = mask_even if (e + k + 1 + colour) % 2 == 0 else mask_odd
                new = jnp.where(mask, new, rows[k + 1])
                if store is None:
                    v_ref[e + k] = new
                else:
                    store(e + k, new)

        blocks(low, count, step, body)

    def first_colour(v_ref, g_ref, refs, low, count, step, sh):
        ri = refs[3]
        mask_even = even(sh)
        mask_odd = jnp.logical_not(mask_even)

        def body(e, step):
            for k in range(step):
                mask = mask_even if (e + k + 1) % 2 == 0 else mask_odd
                v_ref[e + k] = jnp.where(mask, g_ref[e + k] * ri[e + k], 0.0)

        blocks(low, count, step, body)

    def residual_rows(v_ref, g_ref, refs, e, count, sh):
        rows = [v_ref[e - 1 + k] for k in range(count + 2)]
        wests = [None]
        out = []
        for k in range(count):
            total = neighbours(rows, k, e, refs, sh, wests)
            out.append(g_ref[e + k] - (refs[4][e + k] * rows[k + 1] - total))
        return out

    sub_even, lane_even = sub % 2 == 0, lane256 % 2 == 0

    def mean8(t):
        t = t + jnp.where(sub_even, turn(t, -1, 0), turn(t, 1, 0))
        t = t + jnp.where(lane_even, turn(t, -1, 1), turn(t, 1, 1))
        return t * 0.125

    def to_tiles(which):
        a = pairs[:, 0, :] + pairs[:, 2, :]
        b = pairs[:, 4, :] + pairs[:, 6, :]
        stack = jnp.concatenate([*split3(jnp.concatenate([a, b], axis=1)), jnp.zeros((8, 256), F32)], axis=0)
        dots = jnp.dot(stack.astype(jnp.bfloat16), gather[...], preferred_element_type=F32)
        tile = (dots[0:8] + dots[8:16]) + dots[16:24]
        tiles[which, 1] = tile
        tiles[which, 2] = turn(tile, -32, 1)
        tiles[which, 0] = turn(tile, 32, 1)
        tiles_got[which, 2, 1] = tile
        return [
            send(tiles.at[which, 1 + dy], tiles_got.at[which, 2 - dx, 1 - dy], beside(dx, dy))
            for dx, dy in SIDE
        ]

    lanes64 = lanes128 % 64

    def coarse_field(which):
        rows = [
            jnp.where(
                lanes64 < 16, tiles_got[which, g, 0],
                jnp.where(lanes64 < 48, tiles_got[which, g, 1], tiles_got[which, g, 2]),
            )
            for g in range(5)
        ]
        return jnp.concatenate(rows, axis=0)

    def wait(copies):
        for copy in copies:
            copy.wait()

    def coarse_tiles(source_of):
        for c in range(8):
            pairs[c] = source_of(c)

    fine = (wx, wy, wz, inv, diag)
    mid = (wx1, wy1, wz1, inv1, diag1)
    wait(box_copies[0])
    assemble(rho_got, beta, True)
    wait(exchange(0, beta))
    fill(0, beta, True)
    for e in range(1, 41):
        beta1[e] = mean8(beta[2 * e - 1] + beta[2 * e])
    half = 0.5 * 0.0625
    coarse_tiles(lambda c: beta1[13 + 2 * c, :, 0:128] + beta1[14 + 2 * c, :, 0:128])
    tile_copies = to_tiles(0)
    quad_sub, quad_lane = sub // 2 % 2 == 0, lane256 // 2 % 2 == 0
    top, bottom = sub < 4, sub >= 4
    quads = []
    for c in range(-1, 9):
        t = beta1[13 + 2 * c] + beta1[14 + 2 * c]
        t = t + jnp.where(quad_sub, turn(t, -2, 0), turn(t, 2, 0))
        quads.append((t + jnp.where(quad_lane, turn(t, -2, 1), turn(t, 2, 1))) * 0.125)

    def inverse_quad(c):
        b = quads[c + 1]
        north = half * (b + turn(b, -4, 1))
        above = half * (b + jnp.where(top, turn(b, -4, 0), 0.0))
        below = half * (b + jnp.where(bottom, turn(b, 4, 0), 0.0))
        total = half * (b + quads[c + 2]) + half * (quads[c] + b) + north + turn(north, 4, 1) + above + below
        return (2.0 / total)[:, 0:128]

    coarse_tiles(inverse_quad)
    tile_copies += to_tiles(3)
    make_weights(beta, fine, 80, 4, 1, 1.0)
    make_weights(beta1, mid, 40, 4, 2, 0.25)
    rows40, cols40 = iota((40, 128), 0), iota((40, 128), 1) % 64
    at_x, at_y = gx * 8 + rows40 - 16, gy * 32 + cols40 - 16
    in_grid = (at_x >= 0) & (at_x < 8 * nx) & (at_y >= 0) & (at_y < 32 * ny)
    coarse_even = (rows40 + cols40 + iota((40, 128), 1) // 64) % 2 == 0

    wait(box_copies[1])
    assemble(rhs_got, source, False)
    source_copies = exchange(1, source)
    wait(tile_copies)
    b2 = jnp.where(in_grid, coarse_field(0), 0.0)
    wide[0] = half * (b2 + turn(b2, -1, 0))
    wide[1] = half * (b2 + turn(b2, -1, 1))
    wide[2] = half * (b2 + turn(b2, 64, 1))
    wide[3] = jnp.where(in_grid, coarse_field(3), 0.0)
    wait(source_copies)
    fill(1, source, False)

    def to_mid(low, high):
        for e in range(low + 13, high + 13):
            out = residual_rows(phi, source, fine, 2 * e - 1, 2, 1)
            g1[e] = mean8(out[0] + out[1])

    def fine_colour(colour, low, high, cycle):
        if cycle == 0 and colour == 0:
            first_colour(phi, source, fine, low + 25, high - low, 8, 1)
        else:
            colour_step(phi, source, fine, colour, low + 25, high - low, 8, 1)

    def mid_colour(colour, low, high, fresh):
        if fresh and colour == 0:
            first_colour(v1, g1, mid, low + 13, high - low, 8, 2)
        else:
            colour_step(v1, g1, mid, colour, low + 13, high - low, 8, 2)

    for cycle in range(CYCLES):
        reach = 11 if cycle < CYCLES - 1 else 0
        after = (reach + 3) // 2
        before = after + 3
        fine_colour(0, -6, 38, cycle)
        fine_colour(1, -5, 37, cycle)
        to_mid(-2, 18)
        mid_colour(0, -2, 18, True)
        mid_colour(1, -1, 17, True)

        def pair_residual(c):
            out = residual_rows(v1, g1, mid, 13 + 2 * c, 2, 2)
            return (out[0] + out[1])[:, 0:128]

        coarse_tiles(pair_residual)
        tile_copies = to_tiles(1 + cycle)
        outer = 2 * before + 2
        for low, high in ((-outer, -6), (38, 32 + outer)):
            fine_colour(0, low, high, cycle)
        for low, high in ((1 - outer, -5), (37, 31 + outer)):
            fine_colour(1, low, high, cycle)
        for low, high in ((-before, -2), (18, 16 + before)):
            to_mid(low, high)
            mid_colour(0, low, high, True)
        for low, high in ((1 - before, -1), (17, 15 + before)):
            mid_colour(1, low, high, True)
        wait(tile_copies)
        g2 = coarse_field(1 + cycle)
        cx, cy, cz, ci = wide[0], wide[1], wide[2], wide[3]
        v2 = jnp.where(coarse_even, g2 * ci, 0.0)
        for step in range(1, 2 * BOTTOM):
            total = cx * turn(v2, -1, 0) + turn(cx * v2, 1, 0)
            total = total + cy * turn(v2, -1, 1) + turn(cy * v2, 1, 1)
            total = total + cz * turn(v2, 64, 1)
            new = (g2 + total) * ci
            v2 = jnp.where(coarse_even, new, v2) if step % 2 == 0 else jnp.where(coarse_even, v2, new)
        stack = jnp.concatenate(split3(v2[8:40]), axis=0)
        dots = jnp.dot(stack.astype(jnp.bfloat16), spread[...], preferred_element_type=F32)
        grown = (dots[0:32] + dots[32:64]) + dots[64:96]
        depth = (before + 1) // 2
        for c in range(-depth, 8 + depth):
            row = grown[c + 8 : c + 9]
            extra = jnp.where(sub < 4, row[:, 0:256], row[:, 256:512])
            for k in range(2):
                v1[13 + 2 * c + k] = v1[13 + 2 * c + k] + extra
        mid_colour(0, -after - 1, 17 + after, False)
        mid_colour(1, -after, 16 + after, False)
        for e in range(13 - after, 29 + after):
            extra = v1[e]
            for row in (2 * e - 1, 2 * e):
                phi[row] = phi[row] + extra
        fine_colour(0, -reach - 1, 33 + reach, 1)
        if reach:
            fine_colour(1, -reach, 32 + reach, 1)
        else:

            def give(e, value):
                out_ref[e - 25] = value[:, 0:128]

            colour_step(phi, source, fine, 1, 25, 32, 8, 1, give)


def local(nx, ny, send_owner, send_box, rho_old, rhs_old):
    slots = send_owner.shape[2]
    depth, cells = rho_old.shape[3:]
    copies = 3 * (ny - 1) + 2 * 8 + 4 * len(SIDE)

    def vmem(*shape):
        return pltpu.VMEM(shape, F32)

    boxes = vmem(2 * ny, 8, 1024)
    row = pltpu.VMEM((1, 1, slots), I32)
    scratch = [
        row, row, pltpu.VMEM((8, 128), I32),
        vmem(slots, 8, 1024), vmem(slots, 8, 1024), boxes, boxes, boxes, boxes, pltpu.VMEM((ny, 8, 128), I32),
        *[vmem(82, 8, 256)] * 8,
        vmem(2, 2, 8, 8, 128), vmem(2, 2, 20, 8, 128),
        *[vmem(42, 8, 256)] * 8,
        vmem(8, 8, 128), vmem(4, 3, 8, 128), vmem(4, 5, 3, 8, 128),
        pltpu.VMEM((128, 512), jnp.bfloat16), pltpu.VMEM((256, 128), jnp.bfloat16), vmem(4, 40, 128),
        pltpu.SemaphoreType.DMA((4,)), pltpu.SemaphoreType.DMA((copies,)), pltpu.SemaphoreType.DMA((copies,)),
    ]
    out = pl.pallas_call(
        functools.partial(kernel, nx, ny),
        out_shape=jax.ShapeDtypeStruct((32, 8, 128), F32),
        in_specs=[pl.BlockSpec(memory_space=pl.ANY)] * 4,
        out_specs=pl.BlockSpec(memory_space=pltpu.VMEM),
        scratch_shapes=scratch,
        compiler_params=pltpu.CompilerParams(
            collective_id=0, has_side_effects=True, vmem_limit_bytes=int(56 * 1024 * 1024)
        ),
        name="regrid_cycles",
    )(send_owner, send_box, rho_old.reshape(slots, depth, cells), rhs_old.reshape(slots, depth, cells))
    return out.transpose(1, 0, 2)


def solution(mesh):
    placed = (
        P("gx", "gy", None),
        P("gx", "gy", None),
        P("gx", "gy", None, None, None),
        P("gx", "gy", None, None, None),
    )
    return jax.shard_map(
        functools.partial(local, mesh.shape["gx"], mesh.shape["gy"]),
        mesh=mesh, in_specs=placed, out_specs=P(None, "gx", "gy"), check_vma=False,
    )
```

```python
import functools

import jax
import jax.numpy as jnp
from jax import lax
from jax.experimental import pallas as pl
from jax.experimental.pallas import tpu as pltpu
from jax.sharding import PartitionSpec as P

MESH = pl.DeviceIdType.MESH
F32 = jnp.float32
I32 = jnp.int32
CYCLES = 2
BOTTOM = 6
SIDE = [(dx, dy) for dx in (-2, -1, 0, 1, 2) for dy in (-1, 0, 1) if (dx, dy) != (0, 0)]


def iota(shape, dim):
    return lax.broadcasted_iota(I32, shape, dim)


def turn(x, shift, axis):
    return pltpu.roll(x, shift % x.shape[axis], axis)


def split3(x):
    high = x.astype(jnp.bfloat16).astype(F32)
    rest = x - high
    middle = rest.astype(jnp.bfloat16).astype(F32)
    return high, middle, rest - middle


def kernel(
    nx, ny, owner_hbm, box_hbm, rho_hbm, rhs_hbm, out_ref,
    owner_in, box_in, table_ref, rho_in, rhs_in, rho_out, rhs_out, rho_got, rhs_got, tables,
    beta, source, beta1, fine, mid,
    strips, strips_got,
    pairs, tiles, tiles_got, spread, gather, wide,
    in_sem, send_sem, recv_sem,
):
    gx, gy = lax.axis_index("gx"), lax.axis_index("gy")
    ky = 4 if ny % 4 == 0 else ny
    kx = ny // ky

    def beside(dx, dy):
        return (lax.rem(gx + (dx + nx), nx), lax.rem(gy + (dy + ny), ny))

    def mate(o):
        return lax.rem(gy // ky + o // ky, kx) * ky + lax.rem(gy % ky + o % ky, ky)

    used = [0]

    def send(src, dst, device):
        k = used[0]
        used[0] += 1
        copy = pltpu.make_async_remote_copy(
            src_ref=src, dst_ref=dst, send_sem=send_sem.at[k], recv_sem=recv_sem.at[k],
            device_id=device, device_id_type=MESH,
        )
        copy.start()
        return copy

    loads = [
        pltpu.make_async_copy(rho_hbm, rho_in, in_sem.at[0]),
        pltpu.make_async_copy(rhs_hbm, rhs_in, in_sem.at[1]),
        pltpu.make_async_copy(owner_hbm, owner_in, in_sem.at[2]),
        pltpu.make_async_copy(box_hbm, box_in, in_sem.at[3]),
    ]
    for load in loads:
        load.start()

    barrier = pltpu.get_barrier_semaphore()
    peers = [(gx, mate(o)) for o in range(1, ny)] + [beside(dx, dy) for dx, dy in SIDE if dx != 0]
    for device in peers:
        pl.semaphore_signal(barrier, inc=1, device_id=device, device_id_type=MESH)
    slots = owner_in.shape[2]
    table_ref[...] = jnp.full((8, 128), -1, I32)
    loads[2].wait()
    loads[3].wait()
    owner_row = owner_in[0]
    table_ref[0:1, 0:slots] = owner_row
    table_ref[1:2, 0:slots] = box_in[0]
    at_slot = iota((1, slots), 1)
    chosen = []
    for o in range(ny):
        hit = owner_row == mate(o)
        chosen.append((jnp.min(jnp.where(hit, at_slot, slots - 1)), jnp.max(jnp.where(hit, at_slot, 0))))
    pl.semaphore_wait(barrier, len(peers))

    order = sorted(range(1, ny), key=lambda o: (min(o // ky, kx - o // ky) + min(o % ky, ky - o % ky), o))
    table_copies = [send(table_ref, tables.at[o], (gx, mate(o))) for o in order]
    box_copies = []
    for load, held, leaving, arrived in (
        (loads[0], rho_in, rho_out, rho_got),
        (loads[1], rhs_in, rhs_out, rhs_got),
    ):
        load.wait()
        copies = []
        for o in [*order, 0]:
            d = mate(o)
            for r in range(2):
                box = held[chosen[o][r]]
                if o == 0:
                    arrived[r] = box
                else:
                    leaving[2 * o + r] = box
            if o:
                copies.append(
                    send(leaving.at[pl.ds(2 * o, 2)], arrived.at[pl.ds(2 * o, 2)], (gx, d))
                )
        box_copies.append(copies)

    k, n = iota((128, 512), 0), iota((128, 512), 1)
    lane = n % 256
    place = jnp.where(lane < 192, lane // 4 + 16, lane // 4 - 48)
    spread[...] = jnp.where((k // 64 == n // 256) & (k % 64 == place), 1.0, 0.0).astype(jnp.bfloat16)
    k, n = iota((256, 128), 0), iota((256, 128), 1)
    lane = k % 128
    hit = (k // 128 == n // 64) & (lane % 2 == 0) & (lane // 4 + 16 == n % 64)
    gather[...] = jnp.where(hit, 0.125, 0.0).astype(jnp.bfloat16)
    nothing = jnp.zeros((8, 256), F32)
    for ref, last in ((beta, 81), (beta1, 41)):
        ref[0] = nothing
        ref[last] = nothing
    phi0, phi1, source0, source1, *fine = [fine.at[k] for k in range(14)]
    v0, v1, g0, g1, *mid = [mid.at[k] for k in range(14)]
    v0[1] = nothing
    v0[20] = nothing

    lanes128 = iota((8, 128), 1)
    sub, lane256 = iota((8, 256), 0), iota((8, 256), 1)

    tables[0] = table_ref[...]
    for copy in table_copies:
        copy.wait()
    owners, ids = tables[:, 0, :], tables[:, 1, :]
    mine = owners == gy
    slot = iota((ny, 128), 1)
    first = jnp.min(jnp.where(mine, slot, 128), axis=1, keepdims=True)
    index = 2 * iota((ny, 128), 0) + jnp.where(slot == first, 0, 1)
    where_from = [jnp.max(jnp.where(mine & (ids == b), index, 0)) for b in range(4)]

    def assemble(arrived, field, invert):
        for g in range(8):
            parts = [arrived[where_from[b], :, 128 * g : 128 * g + 128] for b in range(4)]
            for r in range(4):
                row = parts[0] if r == 0 else turn(parts[0], -32 * r, 1)
                for b in range(1, 4):
                    moved = parts[b] if b == r else turn(parts[b], 32 * (b - r), 1)
                    row = jnp.where(lanes128 >= 32 * b, moved, row)
                if invert:
                    row = 1.0 / row
                field[25 + 4 * g + r, :, 0:128] = row

    def exchange(which, field):
        left, right = strips.at[which, 0], strips.at[which, 1]
        from_left, from_right = strips_got.at[which, 0], strips_got.at[which, 1]
        main = pl.ds(0, 128)
        copies = [
            send(field.at[pl.ds(33, 24), :, main], field.at[pl.ds(1, 24), :, main], beside(1, 0)),
            send(field.at[pl.ds(25, 24), :, main], field.at[pl.ds(57, 24), :, main], beside(-1, 0)),
        ]
        for j in range(8):
            low = high = None
            for q in range(4):
                row = field[25 + 4 * j + q, :, 0:128]
                a, b = turn(row, 32 * q, 1), turn(row, 32 * q - 96, 1)
                low = a if q == 0 else jnp.where(lanes128 >= 32 * q, a, low)
                high = b if q == 0 else jnp.where(lanes128 >= 32 * q, b, high)
            left[j] = low
            right[j] = high
        for dy, src, dst in ((1, right, from_left), (-1, left, from_right)):
            copies.append(send(src.at[pl.ds(2, 6)], dst.at[pl.ds(0, 6)], beside(1, dy)))
            copies.append(send(src.at[pl.ds(0, 6)], dst.at[pl.ds(14, 6)], beside(-1, dy)))
            copies.append(send(src, dst.at[pl.ds(6, 8)], beside(0, dy)))
        return copies

    row_low, row_high = jnp.where(gx > 0, 1.0, 0.0), jnp.where(gx < nx - 1, 1.0, 0.0)
    lane_low, lane_high = jnp.where(gy > 0, 1.0, 0.0), jnp.where(gy < ny - 1, 1.0, 0.0)
    in_high = lanes128 < 32
    in_low = lanes128 >= 96

    def fill(which, field, put):
        from_left, from_right = strips_got.at[which, 0], strips_got.at[which, 1]
        scale = jnp.where(in_high, lane_high, lane_low)
        for j in range(20):
            a, b = from_left[j], from_right[j]
            for q in range(4):
                low, high = turn(a, 96 - 32 * q, 1), turn(b, -32 * q, 1)
                both = jnp.where(in_high, high, jnp.where(in_low, low, 0.0))
                put(1 + 4 * j + q, field[1 + 4 * j + q, :, 0:128], both)

    edge = jnp.where(in_high, lane_high, lane_low)

    def put_beta(e, main, both):
        if not 25 <= e < 57:
            row_scale = row_low if e < 25 else row_high
            beta[e, :, 0:128] = main * row_scale
            both = both * row_scale
        beta[e, :, 128:256] = both * edge

    even_fine, even_mid = (sub + lane256) % 2 == 0, (sub // 2 + lane256 // 2) % 2 == 0
    held = []

    def put_source(e, main, both):
        held.append(jnp.concatenate([main, both], axis=1))
        if len(held) == 2:
            a, b = held
            source0[e // 2] = jnp.where(even_fine, a, b)
            source1[e // 2] = jnp.where(even_fine, b, a)
            held.clear()

    def make_weights(b_ref, refs, count, sh, even, scale):
        within, x0, x1, y0, y1, z0, z1, i0, i1, d0 = refs
        half = 0.5 * scale
        top, bottom = sub < 8 - sh, sub >= sh
        for p in range(1, count + 1):
            rows = [b_ref[2 * p - 2 + k] for k in range(4)]
            faces = [half * (rows[k] + rows[k + 1]) for k in range(3)]
            norths, ups, totals, inverses = [], [], [], []
            for k in (1, 2):
                b = rows[k]
                north = half * (b + turn(b, -sh, 1))
                above = half * (b + jnp.where(top, turn(b, -sh, 0), 0.0))
                below = half * (b + jnp.where(bottom, turn(b, sh, 0), 0.0))
                total = faces[k] + faces[k - 1] + north + turn(north, sh, 1) + above + below
                inside = b > 0.0
                norths.append(north)
                ups.append(jnp.where(top, above, 0.0))
                totals.append(total)
                inverses.append(jnp.where(inside, 1.0 / jnp.where(inside, total, 1.0), 0.0))
            within[p] = faces[1]
            x0[p] = jnp.where(even, faces[0], faces[2])
            x1[p] = jnp.where(even, faces[2], faces[0])
            for (a, b), first, second in ((norths, y0, y1), (ups, z0, z1), (inverses, i0, i1)):
                first[p] = jnp.where(even, a, b)
                second[p] = jnp.where(even, b, a)
            d0[p] = jnp.where(even, totals[0], totals[1])

    def neighbours(other, colour, p, refs, sh, even):
        within, x0, x1, y0, y1, z0, z1 = refs[:7]
        x, y, z = (x0, y0, z0) if colour == 0 else (x1, y1, z1)
        y_other, z_other = (y1, z1) if colour == 0 else (y0, z0)
        v = other[p]
        before, after = other[p - 1], other[p + 1]
        outside = jnp.where(even, before, after) if colour == 0 else jnp.where(even, after, before)
        total = within[p] * v + x[p] * outside
        total = total + (y[p] * turn(v, -sh, 1) + turn(y_other[p] * v, sh, 1))
        return total + (z[p] * turn(v, -sh, 0) + turn(z_other[p] * v, sh, 0))

    def sweep_colour(fields, sources, refs, colour, low, high, sh, even, store=None):
        field, other = fields[colour], fields[1 - colour]
        for p in range(low, high):
            new = (sources[colour][p] + neighbours(other, colour, p, refs, sh, even)) * refs[7 + colour][p]
            if store is None:
                field[p] = new
            else:
                store(p, new)

    def fresh_colour(fields, sources, refs, low, high):
        for p in range(low, high):
            fields[0][p] = sources[0][p] * refs[7][p]

    def residual(fields, sources, refs, p, sh, even):
        total = neighbours(fields[1], 0, p, refs, sh, even)
        return sources[0][p] - (refs[9][p] * fields[0][p] - total)

    sub_even, lane_even = sub % 2 == 0, lane256 % 2 == 0

    def mean8(t):
        t = t + jnp.where(sub_even, turn(t, -1, 0), turn(t, 1, 0))
        t = t + jnp.where(lane_even, turn(t, -1, 1), turn(t, 1, 1))
        return t * 0.125

    def to_tiles(which):
        a = pairs[:, 0, :] + pairs[:, 2, :]
        b = pairs[:, 4, :] + pairs[:, 6, :]
        stack = jnp.concatenate([*split3(jnp.concatenate([a, b], axis=1)), jnp.zeros((8, 256), F32)], axis=0)
        dots = jnp.dot(stack.astype(jnp.bfloat16), gather[...], preferred_element_type=F32)
        tile = (dots[0:8] + dots[8:16]) + dots[16:24]
        tiles[which, 1] = tile
        tiles[which, 2] = turn(tile, -32, 1)
        tiles[which, 0] = turn(tile, 32, 1)
        tiles_got[which, 2, 1] = tile
        return [
            send(tiles.at[which, 1 + dy], tiles_got.at[which, 2 - dx, 1 - dy], beside(dx, dy))
            for dx, dy in SIDE
        ]

    lanes64 = lanes128 % 64

    def coarse_field(which):
        rows = [
            jnp.where(
                lanes64 < 16, tiles_got[which, g, 0],
                jnp.where(lanes64 < 48, tiles_got[which, g, 1], tiles_got[which, g, 2]),
            )
            for g in range(5)
        ]
        return jnp.concatenate(rows, axis=0)

    def wait(copies):
        for copy in copies:
            copy.wait()

    def coarse_tiles(source_of):
        for c in range(8):
            pairs[c] = source_of(c)

    wait(box_copies[0])
    assemble(rho_got, beta, True)
    wait(exchange(0, beta))
    fill(0, beta, put_beta)
    for e in range(1, 41):
        beta1[e] = mean8(beta[2 * e - 1] + beta[2 * e])
    half = 0.5 * 0.0625
    coarse_tiles(lambda c: beta1[13 + 2 * c, :, 0:128] + beta1[14 + 2 * c, :, 0:128])
    tile_copies = to_tiles(0)
    quad_sub, quad_lane = sub // 2 % 2 == 0, lane256 // 2 % 2 == 0
    top, bottom = sub < 4, sub >= 4
    quads = []
    for c in range(-1, 9):
        t = beta1[13 + 2 * c] + beta1[14 + 2 * c]
        t = t + jnp.where(quad_sub, turn(t, -2, 0), turn(t, 2, 0))
        quads.append((t + jnp.where(quad_lane, turn(t, -2, 1), turn(t, 2, 1))) * 0.125)

    def inverse_quad(c):
        b = quads[c + 1]
        north = half * (b + turn(b, -4, 1))
        above = half * (b + jnp.where(top, turn(b, -4, 0), 0.0))
        below = half * (b + jnp.where(bottom, turn(b, 4, 0), 0.0))
        total = half * (b + quads[c + 2]) + half * (quads[c] + b) + north + turn(north, 4, 1) + above + below
        return (2.0 / total)[:, 0:128]

    coarse_tiles(inverse_quad)
    tile_copies += to_tiles(3)
    make_weights(beta, fine, 40, 1, even_fine, 1.0)
    make_weights(beta1, mid, 20, 2, even_mid, 0.25)
    rows40, cols40 = iota((40, 128), 0), iota((40, 128), 1) % 64
    at_x, at_y = gx * 8 + rows40 - 16, gy * 32 + cols40 - 16
    in_grid = (at_x >= 0) & (at_x < 8 * nx) & (at_y >= 0) & (at_y < 32 * ny)
    coarse_even = (rows40 + cols40 + iota((40, 128), 1) // 64) % 2 == 0

    wait(box_copies[1])
    assemble(rhs_got, source, False)
    source_copies = exchange(1, source)
    wait(tile_copies)
    b2 = jnp.where(in_grid, coarse_field(0), 0.0)
    wide[0] = half * (b2 + turn(b2, -1, 0))
    wide[1] = half * (b2 + turn(b2, -1, 1))
    wide[2] = half * (b2 + turn(b2, 64, 1))
    wide[3] = jnp.where(in_grid, coarse_field(3), 0.0)
    wait(source_copies)
    fill(1, source, put_source)

    phis, sources, vs, gs = (phi0, phi1), (source0, source1), (v0, v1), (g0, g1)

    def to_mid(low, high):
        for p in range(low // 2 + 7, high // 2 + 7):
            a, b = [mean8(residual(phis, sources, fine, 2 * p - 1 + k, 1, even_fine)) for k in range(2)]
            g0[p] = jnp.where(even_mid, a, b)
            g1[p] = jnp.where(even_mid, b, a)

    def fine_colour(colour, low, high, fresh=False, store=None):
        low, high = low // 2 + 13, high // 2 + 13
        if fresh and colour == 0:
            fresh_colour(phis, sources, fine, low, high)
        else:
            sweep_colour(phis, sources, fine, colour, low, high, 1, even_fine, store)

    def mid_colour(colour, low, high, fresh=False):
        low, high = low // 2 + 7, high // 2 + 7
        if fresh:
            fresh_colour(vs, gs, mid, low, high)
        else:
            sweep_colour(vs, gs, mid, colour, low, high, 2, even_mid)

    for cycle in range(CYCLES):
        reach = 11 if cycle < CYCLES - 1 else 0
        after = (reach + 3) // 2
        before = after + 3
        fine_colour(0, -8, 40, cycle == 0)
        fine_colour(1, -6, 38)
        to_mid(-2, 18)
        mid_colour(0, -2, 18, True)
        mid_colour(1, -2, 18)

        def pair_residual(c):
            return residual(vs, gs, mid, 7 + c, 2, even_mid)[:, 0:128]

        coarse_tiles(pair_residual)
        tile_copies = to_tiles(1 + cycle)
        outer = 24 if reach else 10
        inner = outer - 2 if reach else outer
        for low, high in ((-outer, -8), (40, 32 + outer)):
            fine_colour(0, low, high, cycle == 0)
        for low, high in ((-inner, -6), (38, 32 + inner)):
            fine_colour(1, low, high)
        for low, high in ((-before, -2), (18, 16 + before)):
            to_mid(low, high)
            mid_colour(0, low, high, True)
        for low, high in ((-before, 0), (16, 16 + before)):
            mid_colour(1, low, high)
        wait(tile_copies)
        g2 = coarse_field(1 + cycle)
        cx, cy, cz, ci = wide[0], wide[1], wide[2], wide[3]
        v2 = jnp.where(coarse_even, g2 * ci, 0.0)
        for step in range(1, 2 * BOTTOM):
            total = cx * turn(v2, -1, 0) + turn(cx * v2, 1, 0)
            total = total + cy * turn(v2, -1, 1) + turn(cy * v2, 1, 1)
            total = total + cz * turn(v2, 64, 1)
            new = (g2 + total) * ci
            v2 = jnp.where(coarse_even, new, v2) if step % 2 == 0 else jnp.where(coarse_even, v2, new)
        stack = jnp.concatenate(split3(v2[8:40]), axis=0)
        dots = jnp.dot(stack.astype(jnp.bfloat16), spread[...], preferred_element_type=F32)
        grown = (dots[0:32] + dots[32:64]) + dots[64:96]
        depth = (before + 1) // 2
        for c in range(-depth, 8 + depth):
            row = grown[c + 8 : c + 9]
            extra = jnp.where(sub < 4, row[:, 0:256], row[:, 256:512])
            for v in vs:
                v[7 + c] = v[7 + c] + extra
        mid_colour(0, -after - 1, 17 + after)
        mid_colour(1, -after - 1, 17 + after)
        for p in range(7 - (after + 1) // 2, 7 + (17 + after) // 2):
            a, b = v0[p], v1[p]
            for k, extra in ((0, jnp.where(even_mid, a, b)), (1, jnp.where(even_mid, b, a))):
                for phi in phis:
                    phi[2 * p - 1 + k] = phi[2 * p - 1 + k] + extra
        if reach:
            fine_colour(0, -reach - 1, 33 + reach)
            fine_colour(1, -reach - 1, 33 + reach)
        else:

            def give(p, value):
                a, b = phi0[p, :, 0:128], value[:, 0:128]
                out_ref[2 * p - 26] = jnp.where(even_fine[:, 0:128], a, b)
                out_ref[2 * p - 25] = jnp.where(even_fine[:, 0:128], b, a)

            fine_colour(0, -2, 34)
            fine_colour(1, 0, 32, store=give)


def local(nx, ny, send_owner, send_box, rho_old, rhs_old):
    slots = send_owner.shape[2]
    depth, cells = rho_old.shape[3:]
    copies = 3 * (ny - 1) + 2 * 8 + 4 * len(SIDE)

    def vmem(*shape):
        return pltpu.VMEM(shape, F32)

    boxes = vmem(2 * ny, 8, 1024)
    row = pltpu.VMEM((1, 1, slots), I32)
    scratch = [
        row, row, pltpu.VMEM((8, 128), I32),
        vmem(slots, 8, 1024), vmem(slots, 8, 1024), boxes, boxes, boxes, boxes, pltpu.VMEM((ny, 8, 128), I32),
        vmem(82, 8, 256), vmem(82, 8, 256), vmem(42, 8, 256), vmem(14, 42, 8, 256), vmem(14, 22, 8, 256),
        vmem(2, 2, 8, 8, 128), vmem(2, 2, 20, 8, 128),
        vmem(8, 8, 128), vmem(4, 3, 8, 128), vmem(4, 5, 3, 8, 128),
        pltpu.VMEM((128, 512), jnp.bfloat16), pltpu.VMEM((256, 128), jnp.bfloat16), vmem(4, 40, 128),
        pltpu.SemaphoreType.DMA((4,)), pltpu.SemaphoreType.DMA((copies,)), pltpu.SemaphoreType.DMA((copies,)),
    ]
    out = pl.pallas_call(
        functools.partial(kernel, nx, ny),
        out_shape=jax.ShapeDtypeStruct((32, 8, 128), F32),
        in_specs=[pl.BlockSpec(memory_space=pl.ANY)] * 4,
        out_specs=pl.BlockSpec(memory_space=pltpu.VMEM),
        scratch_shapes=scratch,
        compiler_params=pltpu.CompilerParams(
            collective_id=0, has_side_effects=True, vmem_limit_bytes=int(56 * 1024 * 1024)
        ),
        name="regrid_cycles",
    )(send_owner, send_box, rho_old.reshape(slots, depth, cells), rhs_old.reshape(slots, depth, cells))
    return out.transpose(1, 0, 2)


def solution(mesh):
    placed = (
        P("gx", "gy", None),
        P("gx", "gy", None),
        P("gx", "gy", None, None, None),
        P("gx", "gy", None, None, None),
    )
    return jax.shard_map(
        functools.partial(local, mesh.shape["gx"], mesh.shape["gy"]),
        mesh=mesh, in_specs=placed, out_specs=P(None, "gx", "gy"), check_vma=False,
    )
```

```python
import functools

import jax
import jax.numpy as jnp
from jax import lax
from jax.experimental import pallas as pl
from jax.experimental.pallas import tpu as pltpu
from jax.sharding import PartitionSpec as P

MESH = pl.DeviceIdType.MESH
F32 = jnp.float32
I32 = jnp.int32
CYCLES = 2
BOTTOM = 6
SIDE = [(dx, dy) for dx in (-2, -1, 0, 1, 2) for dy in (-1, 0, 1) if (dx, dy) != (0, 0)]


def iota(shape, dim):
    return lax.broadcasted_iota(I32, shape, dim)


def turn(x, shift, axis):
    return pltpu.roll(x, shift % x.shape[axis], axis)


def split3(x):
    high = x.astype(jnp.bfloat16).astype(F32)
    rest = x - high
    middle = rest.astype(jnp.bfloat16).astype(F32)
    return high, middle, rest - middle


def kernel(
    nx, ny, owner_hbm, box_hbm, rho_hbm, rhs_hbm, out_ref,
    owner_in, box_in, table_ref, rho_in, rhs_in, rho_out, rhs_out, rho_got, rhs_got, tables,
    beta, source, beta1, fine, mid,
    strips, strips_got,
    pairs, tiles, tiles_got, spread, gather, wide,
    in_sem, send_sem, recv_sem,
):
    gx, gy = lax.axis_index("gx"), lax.axis_index("gy")
    ky = 4 if ny % 4 == 0 else ny
    kx = ny // ky

    def beside(dx, dy):
        return (lax.rem(gx + (dx + nx), nx), lax.rem(gy + (dy + ny), ny))

    def mate(o):
        return lax.rem(gy // ky + o // ky, kx) * ky + lax.rem(gy % ky + o % ky, ky)

    used = [0]

    def send(src, dst, device):
        k = used[0]
        used[0] += 1
        copy = pltpu.make_async_remote_copy(
            src_ref=src, dst_ref=dst, send_sem=send_sem.at[k], recv_sem=recv_sem.at[k],
            device_id=device, device_id_type=MESH,
        )
        copy.start()
        return copy

    loads = [
        pltpu.make_async_copy(rho_hbm, rho_in, in_sem.at[0]),
        pltpu.make_async_copy(rhs_hbm, rhs_in, in_sem.at[1]),
        pltpu.make_async_copy(owner_hbm, owner_in, in_sem.at[2]),
        pltpu.make_async_copy(box_hbm, box_in, in_sem.at[3]),
    ]
    for load in loads:
        load.start()

    barrier = pltpu.get_barrier_semaphore()
    peers = [(gx, mate(o)) for o in range(1, ny)] + [beside(dx, dy) for dx, dy in SIDE if dx != 0]
    for device in peers:
        pl.semaphore_signal(barrier, inc=1, device_id=device, device_id_type=MESH)
    slots = owner_in.shape[2]
    table_ref[...] = jnp.full((8, 128), -1, I32)
    loads[2].wait()
    loads[3].wait()
    owner_row = owner_in[0]
    table_ref[0:1, 0:slots] = owner_row
    table_ref[1:2, 0:slots] = box_in[0]
    at_slot = iota((1, slots), 1)
    chosen = []
    for o in range(ny):
        hit = owner_row == mate(o)
        chosen.append((jnp.min(jnp.where(hit, at_slot, slots - 1)), jnp.max(jnp.where(hit, at_slot, 0))))
    pl.semaphore_wait(barrier, len(peers))

    order = sorted(range(1, ny), key=lambda o: (min(o // ky, kx - o // ky) + min(o % ky, ky - o % ky), o))
    table_copies = [send(table_ref, tables.at[o], (gx, mate(o))) for o in order]
    box_copies = []
    for load, held, leaving, arrived in (
        (loads[0], rho_in, rho_out, rho_got),
        (loads[1], rhs_in, rhs_out, rhs_got),
    ):
        load.wait()
        copies = []
        for o in [*order, 0]:
            d = mate(o)
            for r in range(2):
                box = held[chosen[o][r]]
                if o == 0:
                    arrived[r] = box
                else:
                    leaving[2 * o + r] = box
            if o:
                copies.append(
                    send(leaving.at[pl.ds(2 * o, 2)], arrived.at[pl.ds(2 * o, 2)], (gx, d))
                )
        box_copies.append(copies)

    k, n = iota((128, 512), 0), iota((128, 512), 1)
    lane = n % 256
    place = jnp.where(lane < 192, lane // 4 + 16, lane // 4 - 48)
    spread[...] = jnp.where((k // 64 == n // 256) & (k % 64 == place), 1.0, 0.0).astype(jnp.bfloat16)
    k, n = iota((256, 128), 0), iota((256, 128), 1)
    lane = k % 128
    hit = (k // 128 == n // 64) & (lane % 2 == 0) & (lane // 4 + 16 == n % 64)
    gather[...] = jnp.where(hit, 0.125, 0.0).astype(jnp.bfloat16)
    nothing = jnp.zeros((8, 256), F32)
    for ref, last in ((beta, 81), (beta1, 41)):
        ref[0] = nothing
        ref[last] = nothing
    phi0, phi1, source0, source1, *fine = [fine.at[k] for k in range(14)]
    v0, v1, g0, g1, *mid = [mid.at[k] for k in range(14)]
    v0[1] = nothing
    v0[20] = nothing

    lanes128 = iota((8, 128), 1)
    sub, lane256 = iota((8, 256), 0), iota((8, 256), 1)

    tables[0] = table_ref[...]
    for copy in table_copies:
        copy.wait()
    owners, ids = tables[:, 0, :], tables[:, 1, :]
    mine = owners == gy
    slot = iota((ny, 128), 1)
    first = jnp.min(jnp.where(mine, slot, 128), axis=1, keepdims=True)
    index = 2 * iota((ny, 128), 0) + jnp.where(slot == first, 0, 1)
    where_from = [jnp.max(jnp.where(mine & (ids == b), index, 0)) for b in range(4)]

    def assemble(arrived, field, invert):
        for g in range(8):
            parts = [arrived[where_from[b], :, 128 * g : 128 * g + 128] for b in range(4)]
            for r in range(4):
                row = parts[0] if r == 0 else turn(parts[0], -32 * r, 1)
                for b in range(1, 4):
                    moved = parts[b] if b == r else turn(parts[b], 32 * (b - r), 1)
                    row = jnp.where(lanes128 >= 32 * b, moved, row)
                if invert:
                    row = 1.0 / row
                field[25 + 4 * g + r, :, 0:128] = row

    def exchange(which, field):
        left, right = strips.at[which, 0], strips.at[which, 1]
        from_left, from_right = strips_got.at[which, 0], strips_got.at[which, 1]
        main = pl.ds(0, 128)
        copies = [
            send(field.at[pl.ds(33, 24), :, main], field.at[pl.ds(1, 24), :, main], beside(1, 0)),
            send(field.at[pl.ds(25, 24), :, main], field.at[pl.ds(57, 24), :, main], beside(-1, 0)),
        ]
        for j in range(8):
            low = high = None
            for q in range(4):
                row = field[25 + 4 * j + q, :, 0:128]
                a, b = turn(row, 32 * q, 1), turn(row, 32 * q - 96, 1)
                low = a if q == 0 else jnp.where(lanes128 >= 32 * q, a, low)
                high = b if q == 0 else jnp.where(lanes128 >= 32 * q, b, high)
            left[j] = low
            right[j] = high
        for dy, src, dst in ((1, right, from_left), (-1, left, from_right)):
            copies.append(send(src.at[pl.ds(2, 6)], dst.at[pl.ds(0, 6)], beside(1, dy)))
            copies.append(send(src.at[pl.ds(0, 6)], dst.at[pl.ds(14, 6)], beside(-1, dy)))
            copies.append(send(src, dst.at[pl.ds(6, 8)], beside(0, dy)))
        return copies

    row_low, row_high = jnp.where(gx > 0, 1.0, 0.0), jnp.where(gx < nx - 1, 1.0, 0.0)
    lane_low, lane_high = jnp.where(gy > 0, 1.0, 0.0), jnp.where(gy < ny - 1, 1.0, 0.0)
    in_high = lanes128 < 32
    in_low = lanes128 >= 96

    def fill(which, field, put):
        from_left, from_right = strips_got.at[which, 0], strips_got.at[which, 1]
        scale = jnp.where(in_high, lane_high, lane_low)
        for j in range(20):
            a, b = from_left[j], from_right[j]
            for q in range(4):
                low, high = turn(a, 96 - 32 * q, 1), turn(b, -32 * q, 1)
                both = jnp.where(in_high, high, jnp.where(in_low, low, 0.0))
                put(1 + 4 * j + q, field[1 + 4 * j + q, :, 0:128], both)

    edge = jnp.where(in_high, lane_high, lane_low)

    def put_beta(e, main, both):
        if not 25 <= e < 57:
            row_scale = row_low if e < 25 else row_high
            beta[e, :, 0:128] = main * row_scale
            both = both * row_scale
        beta[e, :, 128:256] = both * edge

    even_fine, even_mid = (sub + lane256) % 2 == 0, (sub // 2 + lane256 // 2) % 2 == 0
    held = []

    def put_source(e, main, both):
        held.append(jnp.concatenate([main, both], axis=1))
        if len(held) == 2:
            a, b = held
            source0[e // 2] = jnp.where(even_fine, a, b)
            source1[e // 2] = jnp.where(even_fine, b, a)
            held.clear()

    def make_weights(b_ref, refs, count, sh, even, scale):
        within, x0, x1, y0, y1, z0, z1, i0, i1, d0 = refs
        half = 0.5 * scale
        top, bottom = sub < 8 - sh, sub >= sh
        for p in range(1, count + 1):
            rows = [b_ref[2 * p - 2 + k] for k in range(4)]
            faces = [half * (rows[k] + rows[k + 1]) for k in range(3)]
            norths, ups, totals, inverses = [], [], [], []
            for k in (1, 2):
                b = rows[k]
                north = half * (b + turn(b, -sh, 1))
                above = half * (b + jnp.where(top, turn(b, -sh, 0), 0.0))
                below = half * (b + jnp.where(bottom, turn(b, sh, 0), 0.0))
                total = faces[k] + faces[k - 1] + north + turn(north, sh, 1) + above + below
                inside = b > 0.0
                norths.append(north)
                ups.append(jnp.where(top, above, 0.0))
                totals.append(total)
                inverses.append(jnp.where(inside, 1.0 / jnp.where(inside, total, 1.0), 0.0))
            within[p] = faces[1]
            x0[p] = jnp.where(even, faces[0], faces[2])
            x1[p] = jnp.where(even, faces[2], faces[0])
            for (a, b), first, second in ((norths, y0, y1), (ups, z0, z1), (inverses, i0, i1)):
                first[p] = jnp.where(even, a, b)
                second[p] = jnp.where(even, b, a)
            d0[p] = jnp.where(even, totals[0], totals[1])

    def neighbours(other, colour, p, refs, sh, even):
        within, x0, x1, y0, y1, z0, z1 = refs[:7]
        x, y, z = (x0, y0, z0) if colour == 0 else (x1, y1, z1)
        y_other, z_other = (y1, z1) if colour == 0 else (y0, z0)
        v = other[p]
        before, after = other[p - 1], other[p + 1]
        outside = jnp.where(even, before, after) if colour == 0 else jnp.where(even, after, before)
        total = within[p] * v + x[p] * outside
        total = total + (y[p] * turn(v, -sh, 1) + turn(y_other[p] * v, sh, 1))
        return total + (z[p] * turn(v, -sh, 0) + turn(z_other[p] * v, sh, 0))

    def sweep_colour(fields, sources, refs, colour, low, high, sh, even, store=None):
        field, other = fields[colour], fields[1 - colour]
        for p in range(low, high):
            new = (sources[colour][p] + neighbours(other, colour, p, refs, sh, even)) * refs[7 + colour][p]
            if store is None:
                field[p] = new
            else:
                store(p, new)

    def fresh_colour(fields, sources, refs, low, high):
        for p in range(low, high):
            fields[0][p] = sources[0][p] * refs[7][p]

    def residual(fields, sources, refs, p, sh, even):
        total = neighbours(fields[1], 0, p, refs, sh, even)
        return sources[0][p] - (refs[9][p] * fields[0][p] - total)

    sub_even, lane_even = sub % 2 == 0, lane256 % 2 == 0

    def mean8(t):
        t = t + jnp.where(sub_even, turn(t, -1, 0), turn(t, 1, 0))
        t = t + jnp.where(lane_even, turn(t, -1, 1), turn(t, 1, 1))
        return t * 0.125

    def to_tiles(which):
        a = pairs[:, 0, :] + pairs[:, 2, :]
        b = pairs[:, 4, :] + pairs[:, 6, :]
        stack = jnp.concatenate([*split3(jnp.concatenate([a, b], axis=1)), jnp.zeros((8, 256), F32)], axis=0)
        dots = jnp.dot(stack.astype(jnp.bfloat16), gather[...], preferred_element_type=F32)
        tile = (dots[0:8] + dots[8:16]) + dots[16:24]
        tiles[which, 1] = tile
        tiles[which, 2] = turn(tile, -32, 1)
        tiles[which, 0] = turn(tile, 32, 1)
        tiles_got[which, 2, 1] = tile
        return [
            send(tiles.at[which, 1 + dy], tiles_got.at[which, 2 - dx, 1 - dy], beside(dx, dy))
            for dx, dy in SIDE
        ]

    lanes64 = lanes128 % 64

    def coarse_field(which):
        rows = [
            jnp.where(
                lanes64 < 16, tiles_got[which, g, 0],
                jnp.where(lanes64 < 48, tiles_got[which, g, 1], tiles_got[which, g, 2]),
            )
            for g in range(5)
        ]
        return jnp.concatenate(rows, axis=0)

    def wait(copies):
        for copy in copies:
            copy.wait()

    def coarse_tiles(source_of):
        for c in range(8):
            pairs[c] = source_of(c)

    wait(box_copies[0])
    assemble(rho_got, beta, True)
    beta_copies = exchange(0, beta)
    wait(box_copies[1])
    assemble(rhs_got, source, False)
    source_copies = exchange(1, source)
    wait(beta_copies)
    fill(0, beta, put_beta)
    for e in range(1, 41):
        beta1[e] = mean8(beta[2 * e - 1] + beta[2 * e])
    half = 0.5 * 0.0625
    coarse_tiles(lambda c: beta1[13 + 2 * c, :, 0:128] + beta1[14 + 2 * c, :, 0:128])
    weight_copies = to_tiles(0)
    quad_sub, quad_lane = sub // 2 % 2 == 0, lane256 // 2 % 2 == 0
    top, bottom = sub < 4, sub >= 4
    quads = []
    for c in range(-1, 9):
        t = beta1[13 + 2 * c] + beta1[14 + 2 * c]
        t = t + jnp.where(quad_sub, turn(t, -2, 0), turn(t, 2, 0))
        quads.append((t + jnp.where(quad_lane, turn(t, -2, 1), turn(t, 2, 1))) * 0.125)

    def inverse_quad(c):
        b = quads[c + 1]
        north = half * (b + turn(b, -4, 1))
        above = half * (b + jnp.where(top, turn(b, -4, 0), 0.0))
        below = half * (b + jnp.where(bottom, turn(b, 4, 0), 0.0))
        total = half * (b + quads[c + 2]) + half * (quads[c] + b) + north + turn(north, 4, 1) + above + below
        return (2.0 / total)[:, 0:128]

    coarse_tiles(inverse_quad)
    weight_copies += to_tiles(3)
    rows40, cols40 = iota((40, 128), 0), iota((40, 128), 1) % 64
    at_x, at_y = gx * 8 + rows40 - 16, gy * 32 + cols40 - 16
    in_grid = (at_x >= 0) & (at_x < 8 * nx) & (at_y >= 0) & (at_y < 32 * ny)
    coarse_even = (rows40 + cols40 + iota((40, 128), 1) // 64) % 2 == 0

    make_weights(beta, fine, 40, 1, even_fine, 1.0)
    make_weights(beta1, mid, 20, 2, even_mid, 0.25)
    wait(source_copies)
    fill(1, source, put_source)

    phis, sources, vs, gs = (phi0, phi1), (source0, source1), (v0, v1), (g0, g1)

    def to_mid(low, high):
        for p in range(low // 2 + 7, high // 2 + 7):
            a, b = [mean8(residual(phis, sources, fine, 2 * p - 1 + k, 1, even_fine)) for k in range(2)]
            g0[p] = jnp.where(even_mid, a, b)
            g1[p] = jnp.where(even_mid, b, a)

    def fine_colour(colour, low, high, fresh=False, store=None):
        low, high = low // 2 + 13, high // 2 + 13
        if fresh and colour == 0:
            fresh_colour(phis, sources, fine, low, high)
        else:
            sweep_colour(phis, sources, fine, colour, low, high, 1, even_fine, store)

    def mid_colour(colour, low, high, fresh=False):
        low, high = low // 2 + 7, high // 2 + 7
        if fresh:
            fresh_colour(vs, gs, mid, low, high)
        else:
            sweep_colour(vs, gs, mid, colour, low, high, 2, even_mid)

    for cycle in range(CYCLES):
        reach = 11 if cycle < CYCLES - 1 else 0
        after = (reach + 3) // 2
        before = after + 3
        fine_colour(0, -8, 40, cycle == 0)
        fine_colour(1, -6, 38)
        to_mid(-2, 18)
        mid_colour(0, -2, 18, True)
        mid_colour(1, -2, 18)

        def pair_residual(c):
            return residual(vs, gs, mid, 7 + c, 2, even_mid)[:, 0:128]

        coarse_tiles(pair_residual)
        tile_copies = to_tiles(1 + cycle)
        outer = 24 if reach else 10
        inner = outer - 2 if reach else outer
        for low, high in ((-outer, -8), (40, 32 + outer)):
            fine_colour(0, low, high, cycle == 0)
        for low, high in ((-inner, -6), (38, 32 + inner)):
            fine_colour(1, low, high)
        for low, high in ((-before, -2), (18, 16 + before)):
            to_mid(low, high)
            mid_colour(0, low, high, True)
        for low, high in ((-before, 0), (16, 16 + before)):
            mid_colour(1, low, high)
        if cycle == 0:
            wait(weight_copies)
            b2 = jnp.where(in_grid, coarse_field(0), 0.0)
            wide[0] = half * (b2 + turn(b2, -1, 0))
            wide[1] = half * (b2 + turn(b2, -1, 1))
            wide[2] = half * (b2 + turn(b2, 64, 1))
            wide[3] = jnp.where(in_grid, coarse_field(3), 0.0)
        wait(tile_copies)
        g2 = coarse_field(1 + cycle)
        cx, cy, cz, ci = wide[0], wide[1], wide[2], wide[3]
        v2 = jnp.where(coarse_even, g2 * ci, 0.0)
        for step in range(1, 2 * BOTTOM):
            total = cx * turn(v2, -1, 0) + turn(cx * v2, 1, 0)
            total = total + cy * turn(v2, -1, 1) + turn(cy * v2, 1, 1)
            total = total + cz * turn(v2, 64, 1)
            new = (g2 + total) * ci
            v2 = jnp.where(coarse_even, new, v2) if step % 2 == 0 else jnp.where(coarse_even, v2, new)
        stack = jnp.concatenate(split3(v2[8:40]), axis=0)
        dots = jnp.dot(stack.astype(jnp.bfloat16), spread[...], preferred_element_type=F32)
        grown = (dots[0:32] + dots[32:64]) + dots[64:96]
        depth = (before + 1) // 2
        for c in range(-depth, 8 + depth):
            row = grown[c + 8 : c + 9]
            extra = jnp.where(sub < 4, row[:, 0:256], row[:, 256:512])
            for v in vs:
                v[7 + c] = v[7 + c] + extra
        mid_colour(0, -after - 1, 17 + after)
        mid_colour(1, -after - 1, 17 + after)
        for p in range(7 - (after + 1) // 2, 7 + (17 + after) // 2):
            a, b = v0[p], v1[p]
            for k, extra in ((0, jnp.where(even_mid, a, b)), (1, jnp.where(even_mid, b, a))):
                for phi in phis:
                    phi[2 * p - 1 + k] = phi[2 * p - 1 + k] + extra
        if reach:
            fine_colour(0, -reach - 1, 33 + reach)
            fine_colour(1, -reach - 1, 33 + reach)
        else:

            def give(p, value):
                a, b = phi0[p, :, 0:128], value[:, 0:128]
                out_ref[2 * p - 26] = jnp.where(even_fine[:, 0:128], a, b)
                out_ref[2 * p - 25] = jnp.where(even_fine[:, 0:128], b, a)

            fine_colour(0, -2, 34)
            fine_colour(1, 0, 32, store=give)


def local(nx, ny, send_owner, send_box, rho_old, rhs_old):
    slots = send_owner.shape[2]
    depth, cells = rho_old.shape[3:]
    copies = 3 * (ny - 1) + 2 * 8 + 4 * len(SIDE)

    def vmem(*shape):
        return pltpu.VMEM(shape, F32)

    boxes = vmem(2 * ny, 8, 1024)
    row = pltpu.VMEM((1, 1, slots), I32)
    scratch = [
        row, row, pltpu.VMEM((8, 128), I32),
        vmem(slots, 8, 1024), vmem(slots, 8, 1024), boxes, boxes, boxes, boxes, pltpu.VMEM((ny, 8, 128), I32),
        vmem(82, 8, 256), vmem(82, 8, 256), vmem(42, 8, 256), vmem(14, 42, 8, 256), vmem(14, 22, 8, 256),
        vmem(2, 2, 8, 8, 128), vmem(2, 2, 20, 8, 128),
        vmem(8, 8, 128), vmem(4, 3, 8, 128), vmem(4, 5, 3, 8, 128),
        pltpu.VMEM((128, 512), jnp.bfloat16), pltpu.VMEM((256, 128), jnp.bfloat16), vmem(4, 40, 128),
        pltpu.SemaphoreType.DMA((4,)), pltpu.SemaphoreType.DMA((copies,)), pltpu.SemaphoreType.DMA((copies,)),
    ]
    out = pl.pallas_call(
        functools.partial(kernel, nx, ny),
        out_shape=jax.ShapeDtypeStruct((32, 8, 128), F32),
        in_specs=[pl.BlockSpec(memory_space=pl.ANY)] * 4,
        out_specs=pl.BlockSpec(memory_space=pltpu.VMEM),
        scratch_shapes=scratch,
        compiler_params=pltpu.CompilerParams(
            collective_id=0, has_side_effects=True, vmem_limit_bytes=int(56 * 1024 * 1024)
        ),
        name="regrid_cycles",
    )(send_owner, send_box, rho_old.reshape(slots, depth, cells), rhs_old.reshape(slots, depth, cells))
    return out.transpose(1, 0, 2)


def solution(mesh):
    placed = (
        P("gx", "gy", None),
        P("gx", "gy", None),
        P("gx", "gy", None, None, None),
        P("gx", "gy", None, None, None),
    )
    return jax.shard_map(
        functools.partial(local, mesh.shape["gx"], mesh.shape["gy"]),
        mesh=mesh, in_specs=placed, out_specs=P(None, "gx", "gy"), check_vma=False,
    )
```

```python
import functools

import jax
import jax.numpy as jnp
from jax import lax
from jax.experimental import pallas as pl
from jax.experimental.pallas import tpu as pltpu
from jax.sharding import PartitionSpec as P

MESH = pl.DeviceIdType.MESH
F32 = jnp.float32
I32 = jnp.int32
CYCLES = 2
BOTTOM = 6
SIDE = [(-2, -1), (2, 1), (2, -1), (-2, 1), (-1, -1), (1, 1), (1, -1), (-1, 1)]
SIDE += [(0, -1), (0, 1), (-2, 0), (2, 0), (-1, 0), (1, 0)]


def iota(shape, dim):
    return lax.broadcasted_iota(I32, shape, dim)


def turn(x, shift, axis):
    return pltpu.roll(x, shift % x.shape[axis], axis)


def split3(x):
    high = x.astype(jnp.bfloat16).astype(F32)
    rest = x - high
    middle = rest.astype(jnp.bfloat16).astype(F32)
    return high, middle, rest - middle


def kernel(
    nx, ny, owner_hbm, box_hbm, rho_hbm, rhs_hbm, out_ref,
    owner_in, box_in, table_ref, rho_in, rhs_in, rho_out, rhs_out, rho_got, rhs_got, tables,
    beta, source, beta1, fine, mid,
    strips, strips_got,
    pairs, tiles, tiles_got, spread, gather, wide,
    in_sem, send_sem, recv_sem,
):
    gx, gy = lax.axis_index("gx"), lax.axis_index("gy")
    ky = 4 if ny % 4 == 0 else ny
    kx = ny // ky

    def beside(dx, dy):
        return (lax.rem(gx + (dx + nx), nx), lax.rem(gy + (dy + ny), ny))

    def mate(o):
        return lax.rem(gy // ky + o // ky, kx) * ky + lax.rem(gy % ky + o % ky, ky)

    used = [0]

    def send(src, dst, device):
        k = used[0]
        used[0] += 1
        copy = pltpu.make_async_remote_copy(
            src_ref=src, dst_ref=dst, send_sem=send_sem.at[k], recv_sem=recv_sem.at[k],
            device_id=device, device_id_type=MESH,
        )
        copy.start()
        return copy

    loads = [
        pltpu.make_async_copy(rho_hbm, rho_in, in_sem.at[0]),
        pltpu.make_async_copy(rhs_hbm, rhs_in, in_sem.at[1]),
        pltpu.make_async_copy(owner_hbm, owner_in, in_sem.at[2]),
        pltpu.make_async_copy(box_hbm, box_in, in_sem.at[3]),
    ]
    for load in loads:
        load.start()

    barrier = pltpu.get_barrier_semaphore()
    peers = [(gx, mate(o)) for o in range(1, ny)] + [beside(dx, dy) for dx, dy in SIDE if dx != 0]
    for device in peers:
        pl.semaphore_signal(barrier, inc=1, device_id=device, device_id_type=MESH)
    slots = owner_in.shape[2]
    table_ref[...] = jnp.full((8, 128), -1, I32)
    loads[2].wait()
    loads[3].wait()
    owner_row = owner_in[0]
    table_ref[0:1, 0:slots] = owner_row
    table_ref[1:2, 0:slots] = box_in[0]
    at_slot = iota((1, slots), 1)
    chosen = []
    for o in range(ny):
        hit = owner_row == mate(o)
        chosen.append((jnp.min(jnp.where(hit, at_slot, slots - 1)), jnp.max(jnp.where(hit, at_slot, 0))))
    pl.semaphore_wait(barrier, len(peers))

    order = sorted(range(1, ny), key=lambda o: (-min(o // ky, kx - o // ky) - min(o % ky, ky - o % ky), o))
    table_copies = [send(table_ref, tables.at[o], (gx, mate(o))) for o in order]
    box_copies = []
    for load, held, leaving, arrived in (
        (loads[0], rho_in, rho_out, rho_got),
        (loads[1], rhs_in, rhs_out, rhs_got),
    ):
        load.wait()
        copies = []
        for o in [*order, 0]:
            d = mate(o)
            for r in range(2):
                box = held[chosen[o][r]]
                if o == 0:
                    arrived[r] = box
                else:
                    leaving[2 * o + r] = box
            if o:
                copies.append(
                    send(leaving.at[pl.ds(2 * o, 2)], arrived.at[pl.ds(2 * o, 2)], (gx, d))
                )
        box_copies.append(copies)

    k, n = iota((128, 512), 0), iota((128, 512), 1)
    lane = n % 256
    place = jnp.where(lane < 192, lane // 4 + 16, lane // 4 - 48)
    spread[...] = jnp.where((k // 64 == n // 256) & (k % 64 == place), 1.0, 0.0).astype(jnp.bfloat16)
    k, n = iota((256, 128), 0), iota((256, 128), 1)
    lane = k % 128
    hit = (k // 128 == n // 64) & (lane % 2 == 0) & (lane // 4 + 16 == n % 64)
    gather[...] = jnp.where(hit, 0.125, 0.0).astype(jnp.bfloat16)
    nothing = jnp.zeros((8, 256), F32)
    for ref, last in ((beta, 81), (beta1, 41)):
        ref[0] = nothing
        ref[last] = nothing
    phi0, phi1, source0, source1, *fine = [fine.at[k] for k in range(14)]
    v0, v1, g0, g1, *mid = [mid.at[k] for k in range(14)]
    v0[1] = nothing
    v0[20] = nothing

    lanes128 = iota((8, 128), 1)
    sub, lane256 = iota((8, 256), 0), iota((8, 256), 1)

    tables[0] = table_ref[...]
    for copy in table_copies:
        copy.wait()
    owners, ids = tables[:, 0, :], tables[:, 1, :]
    mine = owners == gy
    slot = iota((ny, 128), 1)
    first = jnp.min(jnp.where(mine, slot, 128), axis=1, keepdims=True)
    index = 2 * iota((ny, 128), 0) + jnp.where(slot == first, 0, 1)
    where_from = [jnp.max(jnp.where(mine & (ids == b), index, 0)) for b in range(4)]

    def assemble(arrived, field, invert):
        for g in range(8):
            parts = [arrived[where_from[b], :, 128 * g : 128 * g + 128] for b in range(4)]
            for r in range(4):
                row = parts[0] if r == 0 else turn(parts[0], -32 * r, 1)
                for b in range(1, 4):
                    moved = parts[b] if b == r else turn(parts[b], 32 * (b - r), 1)
                    row = jnp.where(lanes128 >= 32 * b, moved, row)
                if invert:
                    row = 1.0 / row
                field[25 + 4 * g + r, :, 0:128] = row

    def exchange(which, field):
        left, right = strips.at[which, 0], strips.at[which, 1]
        from_left, from_right = strips_got.at[which, 0], strips_got.at[which, 1]
        main = pl.ds(0, 128)
        copies = [
            send(field.at[pl.ds(33, 24), :, main], field.at[pl.ds(1, 24), :, main], beside(1, 0)),
            send(field.at[pl.ds(25, 24), :, main], field.at[pl.ds(57, 24), :, main], beside(-1, 0)),
        ]
        for j in range(8):
            low = high = None
            for q in range(4):
                row = field[25 + 4 * j + q, :, 0:128]
                a, b = turn(row, 32 * q, 1), turn(row, 32 * q - 96, 1)
                low = a if q == 0 else jnp.where(lanes128 >= 32 * q, a, low)
                high = b if q == 0 else jnp.where(lanes128 >= 32 * q, b, high)
            left[j] = low
            right[j] = high
        for dy, src, dst in ((1, right, from_left), (-1, left, from_right)):
            copies.append(send(src.at[pl.ds(2, 6)], dst.at[pl.ds(0, 6)], beside(1, dy)))
            copies.append(send(src.at[pl.ds(0, 6)], dst.at[pl.ds(14, 6)], beside(-1, dy)))
            copies.append(send(src, dst.at[pl.ds(6, 8)], beside(0, dy)))
        return copies

    row_low, row_high = jnp.where(gx > 0, 1.0, 0.0), jnp.where(gx < nx - 1, 1.0, 0.0)
    lane_low, lane_high = jnp.where(gy > 0, 1.0, 0.0), jnp.where(gy < ny - 1, 1.0, 0.0)
    in_high = lanes128 < 32
    in_low = lanes128 >= 96

    def fill(which, field, put):
        from_left, from_right = strips_got.at[which, 0], strips_got.at[which, 1]
        scale = jnp.where(in_high, lane_high, lane_low)
        for j in range(20):
            a, b = from_left[j], from_right[j]
            for q in range(4):
                low, high = turn(a, 96 - 32 * q, 1), turn(b, -32 * q, 1)
                both = jnp.where(in_high, high, jnp.where(in_low, low, 0.0))
                put(1 + 4 * j + q, field[1 + 4 * j + q, :, 0:128], both)

    edge = jnp.where(in_high, lane_high, lane_low)

    def put_beta(e, main, both):
        if not 25 <= e < 57:
            row_scale = row_low if e < 25 else row_high
            beta[e, :, 0:128] = main * row_scale
            both = both * row_scale
        beta[e, :, 128:256] = both * edge

    even_fine, even_mid = (sub + lane256) % 2 == 0, (sub // 2 + lane256 // 2) % 2 == 0
    held = []

    def put_source(e, main, both):
        held.append(jnp.concatenate([main, both], axis=1))
        if len(held) == 2:
            a, b = held
            source0[e // 2] = jnp.where(even_fine, a, b)
            source1[e // 2] = jnp.where(even_fine, b, a)
            held.clear()

    def make_weights(b_ref, refs, count, sh, even, scale):
        within, x0, x1, y0, y1, z0, z1, i0, i1, d0 = refs
        half = 0.5 * scale
        top, bottom = sub < 8 - sh, sub >= sh
        for p in range(1, count + 1):
            rows = [b_ref[2 * p - 2 + k] for k in range(4)]
            faces = [half * (rows[k] + rows[k + 1]) for k in range(3)]
            norths, ups, totals, inverses = [], [], [], []
            for k in (1, 2):
                b = rows[k]
                north = half * (b + turn(b, -sh, 1))
                above = half * (b + jnp.where(top, turn(b, -sh, 0), 0.0))
                below = half * (b + jnp.where(bottom, turn(b, sh, 0), 0.0))
                total = faces[k] + faces[k - 1] + north + turn(north, sh, 1) + above + below
                inside = b > 0.0
                norths.append(north)
                ups.append(jnp.where(top, above, 0.0))
                totals.append(total)
                inverses.append(jnp.where(inside, 1.0 / jnp.where(inside, total, 1.0), 0.0))
            within[p] = faces[1]
            x0[p] = jnp.where(even, faces[0], faces[2])
            x1[p] = jnp.where(even, faces[2], faces[0])
            for (a, b), first, second in ((norths, y0, y1), (ups, z0, z1), (inverses, i0, i1)):
                first[p] = jnp.where(even, a, b)
                second[p] = jnp.where(even, b, a)
            d0[p] = jnp.where(even, totals[0], totals[1])

    def neighbours(other, colour, p, refs, sh, even):
        within, x0, x1, y0, y1, z0, z1 = refs[:7]
        x, y, z = (x0, y0, z0) if colour == 0 else (x1, y1, z1)
        y_other, z_other = (y1, z1) if colour == 0 else (y0, z0)
        v = other[p]
        before, after = other[p - 1], other[p + 1]
        outside = jnp.where(even, before, after) if colour == 0 else jnp.where(even, after, before)
        total = within[p] * v + x[p] * outside
        total = total + (y[p] * turn(v, -sh, 1) + turn(y_other[p] * v, sh, 1))
        return total + (z[p] * turn(v, -sh, 0) + turn(z_other[p] * v, sh, 0))

    def sweep_colour(fields, sources, refs, colour, low, high, sh, even, store=None):
        field, other = fields[colour], fields[1 - colour]
        for p in range(low, high):
            new = (sources[colour][p] + neighbours(other, colour, p, refs, sh, even)) * refs[7 + colour][p]
            if store is None:
                field[p] = new
            else:
                store(p, new)

    def fresh_colour(fields, sources, refs, low, high):
        for p in range(low, high):
            fields[0][p] = sources[0][p] * refs[7][p]

    def residual(fields, sources, refs, p, sh, even):
        total = neighbours(fields[1], 0, p, refs, sh, even)
        return sources[0][p] - (refs[9][p] * fields[0][p] - total)

    sub_even, lane_even = sub % 2 == 0, lane256 % 2 == 0

    def mean8(t):
        t = t + jnp.where(sub_even, turn(t, -1, 0), turn(t, 1, 0))
        t = t + jnp.where(lane_even, turn(t, -1, 1), turn(t, 1, 1))
        return t * 0.125

    def to_tiles(which):
        a = pairs[:, 0, :] + pairs[:, 2, :]
        b = pairs[:, 4, :] + pairs[:, 6, :]
        stack = jnp.concatenate([*split3(jnp.concatenate([a, b], axis=1)), jnp.zeros((8, 256), F32)], axis=0)
        dots = jnp.dot(stack.astype(jnp.bfloat16), gather[...], preferred_element_type=F32)
        tile = (dots[0:8] + dots[8:16]) + dots[16:24]
        tiles[which, 1] = tile
        tiles[which, 2] = turn(tile, -32, 1)
        tiles[which, 0] = turn(tile, 32, 1)
        tiles_got[which, 2, 1] = tile
        return [
            send(tiles.at[which, 1 + dy], tiles_got.at[which, 2 - dx, 1 - dy], beside(dx, dy))
            for dx, dy in SIDE
        ]

    lanes64 = lanes128 % 64

    def coarse_field(which):
        rows = [
            jnp.where(
                lanes64 < 16, tiles_got[which, g, 0],
                jnp.where(lanes64 < 48, tiles_got[which, g, 1], tiles_got[which, g, 2]),
            )
            for g in range(5)
        ]
        return jnp.concatenate(rows, axis=0)

    def wait(copies):
        for copy in copies:
            copy.wait()

    def coarse_tiles(source_of):
        for c in range(8):
            pairs[c] = source_of(c)

    wait(box_copies[0])
    assemble(rho_got, beta, True)
    beta_copies = exchange(0, beta)
    wait(box_copies[1])
    assemble(rhs_got, source, False)
    source_copies = exchange(1, source)
    wait(beta_copies)
    fill(0, beta, put_beta)
    for e in range(1, 41):
        beta1[e] = mean8(beta[2 * e - 1] + beta[2 * e])
    half = 0.5 * 0.0625
    coarse_tiles(lambda c: beta1[13 + 2 * c, :, 0:128] + beta1[14 + 2 * c, :, 0:128])
    weight_copies = to_tiles(0)
    quad_sub, quad_lane = sub // 2 % 2 == 0, lane256 // 2 % 2 == 0
    top, bottom = sub < 4, sub >= 4
    quads = []
    for c in range(-1, 9):
        t = beta1[13 + 2 * c] + beta1[14 + 2 * c]
        t = t + jnp.where(quad_sub, turn(t, -2, 0), turn(t, 2, 0))
        quads.append((t + jnp.where(quad_lane, turn(t, -2, 1), turn(t, 2, 1))) * 0.125)

    def inverse_quad(c):
        b = quads[c + 1]
        north = half * (b + turn(b, -4, 1))
        above = half * (b + jnp.where(top, turn(b, -4, 0), 0.0))
        below = half * (b + jnp.where(bottom, turn(b, 4, 0), 0.0))
        total = half * (b + quads[c + 2]) + half * (quads[c] + b) + north + turn(north, 4, 1) + above + below
        return (2.0 / total)[:, 0:128]

    coarse_tiles(inverse_quad)
    weight_copies += to_tiles(3)
    rows40, cols40 = iota((40, 128), 0), iota((40, 128), 1) % 64
    at_x, at_y = gx * 8 + rows40 - 16, gy * 32 + cols40 - 16
    in_grid = (at_x >= 0) & (at_x < 8 * nx) & (at_y >= 0) & (at_y < 32 * ny)
    coarse_even = (rows40 + cols40 + iota((40, 128), 1) // 64) % 2 == 0

    make_weights(beta, fine, 40, 1, even_fine, 1.0)
    make_weights(beta1, mid, 20, 2, even_mid, 0.25)
    wait(source_copies)
    fill(1, source, put_source)

    phis, sources, vs, gs = (phi0, phi1), (source0, source1), (v0, v1), (g0, g1)

    def to_mid(low, high):
        for p in range(low // 2 + 7, high // 2 + 7):
            a, b = [mean8(residual(phis, sources, fine, 2 * p - 1 + k, 1, even_fine)) for k in range(2)]
            g0[p] = jnp.where(even_mid, a, b)
            g1[p] = jnp.where(even_mid, b, a)

    def fine_colour(colour, low, high, fresh=False, store=None):
        low, high = low // 2 + 13, high // 2 + 13
        if fresh and colour == 0:
            fresh_colour(phis, sources, fine, low, high)
        else:
            sweep_colour(phis, sources, fine, colour, low, high, 1, even_fine, store)

    def mid_colour(colour, low, high, fresh=False):
        low, high = low // 2 + 7, high // 2 + 7
        if fresh:
            fresh_colour(vs, gs, mid, low, high)
        else:
            sweep_colour(vs, gs, mid, colour, low, high, 2, even_mid)

    for cycle in range(CYCLES):
        reach = 11 if cycle < CYCLES - 1 else 0
        after = (reach + 3) // 2
        before = after + 3
        fine_colour(0, -8, 40, cycle == 0)
        fine_colour(1, -6, 38)
        to_mid(-2, 18)
        mid_colour(0, -2, 18, True)
        mid_colour(1, -2, 18)

        def pair_residual(c):
            return residual(vs, gs, mid, 7 + c, 2, even_mid)[:, 0:128]

        coarse_tiles(pair_residual)
        tile_copies = to_tiles(1 + cycle)
        outer = 24 if reach else 10
        inner = outer - 2 if reach else outer
        for low, high in ((-outer, -8), (40, 32 + outer)):
            fine_colour(0, low, high, cycle == 0)
        for low, high in ((-inner, -6), (38, 32 + inner)):
            fine_colour(1, low, high)
        for low, high in ((-before, -2), (18, 16 + before)):
            to_mid(low, high)
            mid_colour(0, low, high, True)
        for low, high in ((-before, 0), (16, 16 + before)):
            mid_colour(1, low, high)
        if cycle == 0:
            wait(weight_copies)
            b2 = jnp.where(in_grid, coarse_field(0), 0.0)
            wide[0] = half * (b2 + turn(b2, -1, 0))
            wide[1] = half * (b2 + turn(b2, -1, 1))
            wide[2] = half * (b2 + turn(b2, 64, 1))
            wide[3] = jnp.where(in_grid, coarse_field(3), 0.0)
        wait(tile_copies)
        g2 = coarse_field(1 + cycle)
        cx, cy, cz, ci = wide[0], wide[1], wide[2], wide[3]
        v2 = jnp.where(coarse_even, g2 * ci, 0.0)
        for step in range(1, 2 * BOTTOM):
            total = cx * turn(v2, -1, 0) + turn(cx * v2, 1, 0)
            total = total + cy * turn(v2, -1, 1) + turn(cy * v2, 1, 1)
            total = total + cz * turn(v2, 64, 1)
            new = (g2 + total) * ci
            v2 = jnp.where(coarse_even, new, v2) if step % 2 == 0 else jnp.where(coarse_even, v2, new)
        stack = jnp.concatenate(split3(v2[8:40]), axis=0)
        dots = jnp.dot(stack.astype(jnp.bfloat16), spread[...], preferred_element_type=F32)
        grown = (dots[0:32] + dots[32:64]) + dots[64:96]
        depth = (before + 1) // 2
        for c in range(-depth, 8 + depth):
            row = grown[c + 8 : c + 9]
            extra = jnp.where(sub < 4, row[:, 0:256], row[:, 256:512])
            for v in vs:
                v[7 + c] = v[7 + c] + extra
        mid_colour(0, -after - 1, 17 + after)
        mid_colour(1, -after - 1, 17 + after)
        for p in range(7 - (after + 1) // 2, 7 + (17 + after) // 2):
            a, b = v0[p], v1[p]
            for k, extra in ((0, jnp.where(even_mid, a, b)), (1, jnp.where(even_mid, b, a))):
                for phi in phis:
                    phi[2 * p - 1 + k] = phi[2 * p - 1 + k] + extra
        if reach:
            fine_colour(0, -reach - 1, 33 + reach)
            fine_colour(1, -reach - 1, 33 + reach)
        else:

            def give(p, value):
                a, b = phi0[p, :, 0:128], value[:, 0:128]
                out_ref[2 * p - 26] = jnp.where(even_fine[:, 0:128], a, b)
                out_ref[2 * p - 25] = jnp.where(even_fine[:, 0:128], b, a)

            fine_colour(0, -2, 34)
            fine_colour(1, 0, 32, store=give)


def local(nx, ny, send_owner, send_box, rho_old, rhs_old):
    slots = send_owner.shape[2]
    depth, cells = rho_old.shape[3:]
    copies = 3 * (ny - 1) + 2 * 8 + 4 * len(SIDE)

    def vmem(*shape):
        return pltpu.VMEM(shape, F32)

    boxes = vmem(2 * ny, 8, 1024)
    row = pltpu.VMEM((1, 1, slots), I32)
    scratch = [
        row, row, pltpu.VMEM((8, 128), I32),
        vmem(slots, 8, 1024), vmem(slots, 8, 1024), boxes, boxes, boxes, boxes, pltpu.VMEM((ny, 8, 128), I32),
        vmem(82, 8, 256), vmem(82, 8, 256), vmem(42, 8, 256), vmem(14, 42, 8, 256), vmem(14, 22, 8, 256),
        vmem(2, 2, 8, 8, 128), vmem(2, 2, 20, 8, 128),
        vmem(8, 8, 128), vmem(4, 3, 8, 128), vmem(4, 5, 3, 8, 128),
        pltpu.VMEM((128, 512), jnp.bfloat16), pltpu.VMEM((256, 128), jnp.bfloat16), vmem(4, 40, 128),
        pltpu.SemaphoreType.DMA((4,)), pltpu.SemaphoreType.DMA((copies,)), pltpu.SemaphoreType.DMA((copies,)),
    ]
    out = pl.pallas_call(
        functools.partial(kernel, nx, ny),
        out_shape=jax.ShapeDtypeStruct((32, 8, 128), F32),
        in_specs=[pl.BlockSpec(memory_space=pl.ANY)] * 4,
        out_specs=pl.BlockSpec(memory_space=pltpu.VMEM),
        scratch_shapes=scratch,
        compiler_params=pltpu.CompilerParams(
            collective_id=0, has_side_effects=True, vmem_limit_bytes=int(56 * 1024 * 1024)
        ),
        name="regrid_cycles",
    )(send_owner, send_box, rho_old.reshape(slots, depth, cells), rhs_old.reshape(slots, depth, cells))
    return out.transpose(1, 0, 2)


def solution(mesh):
    placed = (
        P("gx", "gy", None),
        P("gx", "gy", None),
        P("gx", "gy", None, None, None),
        P("gx", "gy", None, None, None),
    )
    return jax.shard_map(
        functools.partial(local, mesh.shape["gx"], mesh.shape["gy"]),
        mesh=mesh, in_specs=placed, out_specs=P(None, "gx", "gy"), check_vma=False,
    )
```
